512 devices in a mesh: nodes: 64 (over y_hi, z, core), heads: 8 (over x, y_lo).
Axes of the slice: x: 4, y: 8 (y_hi: 4, y_lo: 2; y = y_hi * 2 + y_lo), z: 8, core: 2. Of those that a mesh axis runs over, the one named last changes fastest.
Arguments:
- inputs: bfloat16 [16384, 1024], P('nodes', 'heads'), may hold values from -6 to 6
- out_grad: bfloat16 [16384, 1024], P('nodes', 'heads'), may hold values from -6 to 6
- w_query: bfloat16 [1024, 1024], P(None, 'heads'), may hold values from -0.1875 to 0.1875
- w_key: bfloat16 [1024, 1024], P(None, 'heads'), may hold values from -0.1875 to 0.1875
- w_value: bfloat16 [1024, 1024], P(None, 'heads'), may hold values from -0.1875 to 0.1875
- w_out: bfloat16 [1024, 1024], P('heads'), may hold values from -0.1875 to 0.1875
- live_rows: int32 [64], P('nodes'), may hold values from 85 to 256, as said below
- window_blocks: int32 [128, 3], P('nodes'), may hold values from 0 to 127, as said below
Outputs:
- input_grad: bfloat16 [16384, 1024], P('nodes', 'heads')
- grad_query: bfloat16 [1024, 1024], P(None, 'heads')
- grad_key: bfloat16 [1024, 1024], P(None, 'heads')
- grad_value: bfloat16 [1024, 1024], P(None, 'heads')
- grad_out: bfloat16 [1024, 1024], P('heads')
The draws below stay inside these ranges and needn't reach their ends.
Inputs may be any that keep to these rules, and one draw needn't show every extreme that they name: `live_rows`: partition 0 and one other partition are full in every draw. `window_blocks`: entry 0 of block b's window is b itself; the other entries are distinct blocks other than b within 2 blocks of b.
All inputs are finite; a program needn't handle non-finite values.
Results may differ from the reference program's by a relative error of at most 0.012.
Values may be sent and summed in bfloat16 or wider, within the bound.
A program may use at most 64 MiB of HBM per device.

```python
import jax
import jax.numpy as jnp
from jax import lax

D = 1024
HEADS = 16
HEAD_DIM = 64
BLOCK = 128
HALO_BLOCKS = 2
WINDOW = 3
ROWS_DEV = 256
PARTITIONS = 64
NBLK = 128
NODES = 16384


def draw_live_rows(key, part):
    key = jax.random.fold_in(key, 12)
    counts = jax.random.randint(key, (PARTITIONS,), ROWS_DEV // 3, ROWS_DEV + 1)
    filled = jax.random.randint(jax.random.fold_in(key, 1), (), 1, PARTITIONS)
    indices = jnp.arange(PARTITIONS)
    full = (indices == filled) | (indices == 0)
    return jnp.where(full, ROWS_DEV, counts).astype(jnp.int32)


def draw_window_blocks(key, part):
    key = jax.random.fold_in(key, 11)
    offsets = jnp.concatenate([jnp.arange(-HALO_BLOCKS, 0), jnp.arange(1, HALO_BLOCKS + 1)])
    base_ids = jnp.arange(NBLK)[:, None]
    candidate = base_ids + offsets[None, :]
    usable = (candidate >= 0) & (candidate < NBLK)
    priority = jax.random.randint(key, (NBLK, 2 * HALO_BLOCKS), 0, 1000) * (2 * HALO_BLOCKS) + jnp.arange(2 * HALO_BLOCKS)[None, :]
    priority = jnp.where(usable, priority, -1)
    unused, picked = lax.top_k(priority, WINDOW - 1)
    chosen = jnp.take_along_axis(candidate, picked, 1)
    return jnp.concatenate([base_ids, chosen], 1).astype(jnp.int32)


def level_of(rng, dims, cuts, low, top_value):
    factor_of = 1.0
    for dim, shards_of in cuts:
        steps = jax.random.uniform(jax.random.fold_in(jax.random.fold_in(rng, 6), dim), (shards_of,), jnp.float32, low / len(cuts), top_value / len(cuts))
        factor_of = factor_of * jnp.repeat(jnp.exp(steps), dims[dim] // shards_of).reshape((-1,) + (1,) * (len(dims) - 1 - dim))
    return factor_of


def scatter_about(stream_key, dims, width, reach, cuts=(), kind=jnp.bfloat16):
    drawn = width * jax.random.normal(stream_key, dims, jnp.float32)
    if cuts:
        drawn = drawn * level_of(stream_key, dims, cuts, -0.22, 0.18)
    return jnp.clip(drawn, -reach, reach).astype(kind)


def setup_inputs(seed: int = 0) -> dict:
    arg_keys = jax.random.split(jax.random.key(seed), 9)
    inputs = scatter_about(arg_keys[0], (NODES, D), 1.0, 6.0, ((0, 64), (1, 8)))
    out_grad = scatter_about(arg_keys[1], (NODES, D), 1.0, 6.0, ((0, 64), (1, 8)))
    w_query = scatter_about(arg_keys[2], (D, D), D ** -0.5, 0.1875, ((1, 8),))
    w_key = scatter_about(arg_keys[3], (D, D), D ** -0.5, 0.1875, ((1, 8),))
    w_value = scatter_about(arg_keys[4], (D, D), D ** -0.5, 0.1875, ((1, 8),))
    w_out = scatter_about(arg_keys[5], (D, D), D ** -0.5, 0.1875, ((0, 8),))
    live_rows = draw_live_rows(jax.random.fold_in(arg_keys[8], 71), 0)
    window_blocks = draw_window_blocks(jax.random.fold_in(arg_keys[8], 71), 0)
    return dict(inputs=inputs, out_grad=out_grad, w_query=w_query, w_key=w_key, w_value=w_value, w_out=w_out, live_rows=live_rows, window_blocks=window_blocks)


def reference(inputs, out_grad, w_query, w_key, w_value, w_out, live_rows, window_blocks):
    scale = HEAD_DIM ** -0.5
    row_ids = jnp.arange(NODES, dtype=jnp.int32)
    owners = row_ids // ROWS_DEV
    row_live = (row_ids - owners * ROWS_DEV) < live_rows[owners]
    queries = jnp.dot(inputs, w_query, preferred_element_type=jnp.float32).astype(jnp.bfloat16)
    keys_all = jnp.dot(inputs, w_key, preferred_element_type=jnp.float32).astype(jnp.bfloat16)
    values_all = jnp.dot(inputs, w_value, preferred_element_type=jnp.float32).astype(jnp.bfloat16)
    back = jnp.dot(out_grad, w_out.T, preferred_element_type=jnp.float32).astype(jnp.bfloat16)
    shape4 = (NBLK, BLOCK, HEADS, HEAD_DIM)
    q_blocks = queries.reshape(shape4)
    k_blocks = keys_all.reshape(shape4)
    v_blocks = values_all.reshape(shape4)
    g_blocks = back.reshape(shape4)
    live_blocks = row_live.reshape(NBLK, BLOCK)
    local_ids = jnp.arange(BLOCK, dtype=jnp.int32)

    def step(carry, block_id):
        key_acc, val_acc = carry
        chosen = window_blocks[block_id].astype(jnp.int32)
        key_sel = k_blocks[chosen].reshape(WINDOW * BLOCK, HEADS, HEAD_DIM).astype(jnp.float32)
        val_sel = v_blocks[chosen].reshape(WINDOW * BLOCK, HEADS, HEAD_DIM).astype(jnp.float32)
        query_blk = q_blocks[block_id].astype(jnp.float32)
        back_blk = g_blocks[block_id].astype(jnp.float32)
        key_rows = (chosen[:, None] * BLOCK + local_ids[None, :]).reshape(-1)
        query_rows = block_id * BLOCK + local_ids
        allowed = live_blocks[chosen].reshape(-1)[None, :] | (key_rows[None, :] == query_rows[:, None])
        scores = jnp.einsum('qhd,khd->hqk', query_blk, key_sel) * scale
        expo = jnp.where(allowed[None], jnp.exp(scores), 0.0)
        probs = expo / jnp.sum(expo, -1, keepdims=True)
        probs_low = lax.optimization_barrier(probs.astype(jnp.bfloat16)).astype(jnp.float32)
        attended = jnp.einsum('hqk,khd->qhd', probs_low, val_sel)
        dprob = jnp.einsum('qhd,khd->hqk', back_blk, val_sel)
        delta = jnp.sum(probs * dprob, -1, keepdims=True)
        dscore = lax.optimization_barrier((scale * probs * (dprob - delta)).astype(jnp.bfloat16)).astype(jnp.float32)
        dquery = jnp.einsum('hqk,khd->qhd', dscore, key_sel)
        dkey = jnp.einsum('hqk,qhd->khd', dscore, query_blk).reshape(WINDOW, BLOCK, HEADS, HEAD_DIM)
        dval = jnp.einsum('hqk,qhd->khd', probs_low, back_blk).reshape(WINDOW, BLOCK, HEADS, HEAD_DIM)
        key_acc = key_acc.at[chosen].add(dkey)
        val_acc = val_acc.at[chosen].add(dval)
        return (key_acc, val_acc), (attended, dquery)

    zeros = jnp.zeros(shape4, jnp.float32)
    (key_acc, val_acc), (attended, dquery) = lax.scan(step, (zeros, zeros), jnp.arange(NBLK, dtype=jnp.int32))
    attn_low = attended.reshape(NODES, D).astype(jnp.bfloat16)
    dq_low = dquery.reshape(NODES, D).astype(jnp.bfloat16)
    dk_low = key_acc.reshape(NODES, D).astype(jnp.bfloat16)
    dv_low = val_acc.reshape(NODES, D).astype(jnp.bfloat16)
    input_grad = (jnp.dot(dq_low, w_query.T, preferred_element_type=jnp.float32)
                  + jnp.dot(dk_low, w_key.T, preferred_element_type=jnp.float32)
                  + jnp.dot(dv_low, w_value.T, preferred_element_type=jnp.float32)).astype(jnp.bfloat16)
    grad_query = jnp.dot(inputs.T, dq_low, preferred_element_type=jnp.float32).astype(jnp.bfloat16)
    grad_key = jnp.dot(inputs.T, dk_low, preferred_element_type=jnp.float32).astype(jnp.bfloat16)
    grad_value = jnp.dot(inputs.T, dv_low, preferred_element_type=jnp.float32).astype(jnp.bfloat16)
    grad_out = jnp.dot(attn_low.T, out_grad, preferred_element_type=jnp.float32).astype(jnp.bfloat16)
    return (input_grad, grad_query, grad_key, grad_value, grad_out)
```

```python
import functools

import jax
import jax.numpy as jnp
from jax import lax
from jax.experimental import pallas as pl
from jax.experimental.pallas import tpu as pltpu
from jax.sharding import PartitionSpec as P

HEAD_DIM = 64
BLOCK = 128
REACH = 5
ROWS = 256
COLS = 128
SHARDS = 8
NZ = 8
NY = 4
SCALE = HEAD_DIM ** (-0.5)
BF = jnp.bfloat16
F32 = jnp.float32
MESH = pl.DeviceIdType.MESH
NT = (((1,), (1,)), ((), ()))
TN = (((0,), (0,)), ((), ()))


def mm(a, b):
    return jnp.dot(a, b, preferred_element_type=F32)


def mm_nt(a, b):
    return lax.dot_general(a, b, NT, preferred_element_type=F32)


def mm_tn(a, b):
    return lax.dot_general(a, b, TN, preferred_element_type=F32)


class Copies:
    def __init__(self, send, recv):
        self.send, self.recv, self.used, self.started = send, recv, 0, []

    def remote(self, src, dst, device):
        i = self.used
        self.used += 1
        copy = pltpu.make_async_remote_copy(
            src_ref=src,
            dst_ref=dst,
            send_sem=self.send.at[i],
            recv_sem=self.recv.at[i],
            device_id=device,
            device_id_type=MESH,
        )
        copy.start()
        self.started.append(copy)
        return copy


def kernel(
    x_in, g_in, wq_in, wk_in, wv_in, wo_in, live_in, win_in,
    ig_out, f_out,
    xg, gg, wqkv, wo, kv, qm, bm, probs, attn, dq, dkv_ext, dkv_send, dkv_recv, grads,
    terms, core_recv, part, ra1, rb1, sa, sb, ra2, rb2, fin, it_send, it_recv, ig,
    local_sem, send_sem, recv_sem, out_sem,
):
    node = lax.axis_index("nodes")
    head = lax.axis_index("heads")
    core = lax.rem(node, 2)
    z = lax.rem(node // 2, NZ)
    y = node // (2 * NZ)
    nodes = 2 * NZ * NY

    def at_head(d):
        return lax.rem(head + d, SHARDS)

    def at_z(d):
        return lax.rem(z + d, NZ)

    def at_y(d):
        return lax.rem(y + d, NY)

    left = (lax.rem(node + nodes - 1, nodes), head)
    right = (lax.rem(node + 1, nodes), head)
    other = (node + 1 - 2 * core, head)

    def z_dev(d):
        return ((y * NZ + at_z(d)) * 2 + core, head)

    def y_dev(d):
        return ((at_y(d) * NZ + z) * 2 + core, head)

    def head_dev(d):
        return (node, at_head(d))

    partners = [left, right]
    partners += [head_dev(d) for d in range(1, SHARDS)]
    partners += [z_dev(d) for d in range(1, NZ)]
    partners += [y_dev(d) for d in range(1, NY)]
    barrier = pltpu.get_barrier_semaphore()
    for dev in partners:
        pl.semaphore_signal(barrier, inc=1, device_id=dev, device_id_type=MESH)

    loads = [
        pltpu.make_async_copy(x_in, xg.at[head], local_sem.at[0]),
        pltpu.make_async_copy(wq_in, wqkv.at[:, 0:COLS], local_sem.at[1]),
        pltpu.make_async_copy(wk_in, wqkv.at[:, COLS : 2 * COLS], local_sem.at[2]),
        pltpu.make_async_copy(wv_in, wqkv.at[:, 2 * COLS : 3 * COLS], local_sem.at[3]),
        pltpu.make_async_copy(g_in, gg.at[head], local_sem.at[4]),
        pltpu.make_async_copy(wo_in, wo, local_sem.at[5]),
    ]
    for load in loads:
        load.start()

    pl.semaphore_wait(barrier, len(partners))
    copies = Copies(send_sem, recv_sem)
    x_copies = [copies.remote(x_in, xg.at[head], head_dev(d)) for d in range(1, SHARDS)]
    g_copies = [copies.remote(g_in, gg.at[head], head_dev(d)) for d in range(1, SHARDS)]

    live = live_in[0]
    lane_row = lax.broadcasted_iota(jnp.int32, (16, ROWS), 1)
    kv[1, ROWS : ROWS + 16, :] = jnp.where(lane_row < live, 1.0, 0.0).astype(BF)

    for load in loads:
        load.wait()
    for copy in x_copies:
        copy.wait_recv()

    x_full = jnp.concatenate([xg[s] for s in range(SHARDS)], axis=1)
    kv[1, 0:ROWS, :] = mm(x_full, wqkv[:, COLS:]).astype(BF)
    kv_right = copies.remote(kv.at[1], kv.at[0], right)
    kv_left = copies.remote(kv.at[1], kv.at[2], left)

    first = lax.broadcasted_iota(jnp.int32, (ROWS, COLS), 1) < HEAD_DIM
    queries = mm(x_full, wqkv[:, 0:COLS])
    qm[0] = jnp.where(first, queries, 0.0).astype(BF)
    qm[1] = jnp.where(first, 0.0, queries).astype(BF)

    kv_right.wait_recv()
    kv_left.wait_recv()

    def reach(b, lo):
        return jnp.concatenate(
            [
                kv[e // 2, (e % 2) * BLOCK : (e % 2 + 1) * BLOCK, lo : lo + COLS]
                for e in range(b, b + REACH)
            ],
            axis=0,
        )

    live_ext = jnp.concatenate([kv[i, ROWS : ROWS + 16, :] for i in range(3)], axis=1)
    live_ext = live_ext.astype(F32)[0:1, :]
    first_b = first[0:BLOCK]
    span = REACH * BLOCK
    col = lax.broadcasted_iota(jnp.int32, (BLOCK, span), 1)
    row = lax.broadcasted_iota(jnp.int32, (BLOCK, span), 0)
    diag = col == row + 2 * BLOCK
    for b in range(2):
        rows = slice(b * BLOCK, (b + 1) * BLOCK)
        keys, vals = reach(b, 0), reach(b, COLS)
        block = lax.broadcasted_iota(jnp.int32, (1, span), 1) // BLOCK + (2 * node - 2 + b)
        chosen = (block == win_in[b, 0]) | (block == win_in[b, 1]) | (block == win_in[b, 2])
        usable = jnp.where(chosen, live_ext[:, b * BLOCK : b * BLOCK + span], 0.0)
        allowed = diag | (jnp.broadcast_to(usable, (BLOCK, span)) > 0.5)
        outs = []
        for h in range(2):
            scores = mm_nt(qm[h, rows, :], keys) * SCALE
            expo = jnp.where(allowed, jnp.exp(scores), 0.0)
            prob = expo / jnp.sum(expo, axis=-1, keepdims=True)
            probs[2 * b + h] = prob
            outs.append(mm(prob.astype(BF), vals))
        attn[rows, :] = jnp.where(first_b, outs[0], outs[1]).astype(BF)

    for copy in g_copies:
        copy.wait_recv()
    g_full = jnp.concatenate([gg[s] for s in range(SHARDS)], axis=1)
    back = mm_nt(g_full, wo[...])
    bm[0] = jnp.where(first, back, 0.0).astype(BF)
    bm[1] = jnp.where(first, 0.0, back).astype(BF)

    for b in range(2):
        rows = slice(b * BLOCK, (b + 1) * BLOCK)
        keys, vals = reach(b, 0), reach(b, COLS)
        outs, dk, dv = [], 0.0, 0.0
        for h in range(2):
            prob = probs[2 * b + h]
            dprob = mm_nt(bm[h, rows, :], vals)
            delta = jnp.sum(prob * dprob, axis=-1, keepdims=True)
            dscore = (SCALE * prob * (dprob - delta)).astype(BF)
            outs.append(mm(dscore, keys))
            dk = dk + mm_tn(dscore, qm[h, rows, :])
            dv = dv + mm_tn(prob.astype(BF), bm[h, rows, :])
        dq[rows, :] = jnp.where(first_b, outs[0], outs[1]).astype(BF)
        if b == 0:
            dkv_ext[0:span, 0:COLS] = dk
            dkv_ext[0:span, COLS:] = dv
        else:
            dkv_ext[BLOCK:span, 0:COLS] += dk[0 : span - BLOCK]
            dkv_ext[BLOCK:span, COLS:] += dv[0 : span - BLOCK]
            dkv_ext[span:, 0:COLS] = dk[span - BLOCK :]
            dkv_ext[span:, COLS:] = dv[span - BLOCK :]

    dkv_send[0] = dkv_ext[0:ROWS, :].astype(BF)
    dkv_send[1] = dkv_ext[2 * ROWS :, :].astype(BF)
    dkv_left = copies.remote(dkv_send.at[0], dkv_recv.at[0], left)
    dkv_right = copies.remote(dkv_send.at[1], dkv_recv.at[1], right)

    for s in range(SHARDS):
        terms[0, s] = mm_tn(xg[s], dq[...]).astype(BF)
        terms[1, s] = mm_tn(attn[...], gg[s]).astype(BF)
    core_copies = [copies.remote(terms.at[1 - core], core_recv.at[0], other)]

    dkv_left.wait_recv()
    dkv_right.wait_recv()
    dkv = dkv_ext[ROWS : 2 * ROWS, :] + dkv_recv[0].astype(F32) + dkv_recv[1].astype(F32)
    grads[:, 0:COLS] = dq[...]
    grads[:, COLS:] = dkv.astype(BF)
    for s in range(SHARDS):
        both = mm_tn(xg[s], grads[:, COLS:]).astype(BF)
        terms[2, s] = both[:, 0:COLS]
        terms[3, s] = both[:, COLS:]
    core_copies.append(copies.remote(terms.at[3 - core], core_recv.at[1], other))

    half, piece = BLOCK // 2, BLOCK // 8

    def low(i):
        return pl.ds(pl.multiple_of(i * piece, piece), piece)

    def high(i):
        return pl.ds(pl.multiple_of(half + i * piece, piece), piece)

    def first_reduce(e):
        core_copies[e].wait_recv()
        own = terms[2 * e + core].astype(F32) + core_recv[e].astype(F32)
        part[e] = own.astype(BF)
        a = [
            copies.remote(part.at[e, at_z(d), 0:half, :], ra1.at[e, d], z_dev(d))
            for d in range(1, NZ)
        ]
        b = [
            copies.remote(part.at[e, :, high(at_y(d)), :], rb1.at[e, d], y_dev(d))
            for d in range(1, NY)
        ]
        return a, b

    def second_reduce(e, a, b):
        for copy in a:
            copy.wait_recv()
        total = part[e, z, 0:half, :].astype(F32)
        for d in range(1, NZ):
            total = total + ra1[e, d].astype(F32)
        sa[e] = total.astype(BF)
        a = [copies.remote(sa.at[e, low(at_y(d)), :], ra2.at[e, d], y_dev(d)) for d in range(1, NY)]
        for copy in b:
            copy.wait_recv()
        total = part[e, :, high(y), :].astype(F32)
        for d in range(1, NY):
            total = total + rb1[e, d].astype(F32)
        sb[e] = total.astype(BF)
        b = [copies.remote(sb.at[e, at_z(d)], rb2.at[e, d], z_dev(d)) for d in range(1, NZ)]
        return a, b

    def first_gather(e, a, b):
        mine = 2 * e + core
        for copy in a:
            copy.wait_recv()
        total = sa[e, low(y), :].astype(F32)
        for d in range(1, NY):
            total = total + ra2[e, d].astype(F32)
        fin[mine, z, low(y), :] = total.astype(BF)
        ref = fin.at[mine, z, low(y), :]
        a = [copies.remote(ref, ref, y_dev(d)) for d in range(1, NY)]
        for copy in b:
            copy.wait_recv()
        total = sb[e, z].astype(F32)
        for d in range(1, NZ):
            total = total + rb2[e, d].astype(F32)
        fin[mine, z, high(y), :] = total.astype(BF)
        ref = fin.at[mine, z, high(y), :]
        b = [copies.remote(ref, ref, z_dev(d)) for d in range(1, NZ)]
        return a, b

    def second_gather(e, a, b):
        mine = 2 * e + core
        for copy in a:
            copy.wait_recv()
        ref = fin.at[mine, z, 0:half, :]
        a = [copies.remote(ref, ref, z_dev(d)) for d in range(1, NZ)]
        for copy in b:
            copy.wait_recv()
        ref = fin.at[mine, :, high(y), :]
        b = [copies.remote(ref, ref, y_dev(d)) for d in range(1, NY)]
        return a, b

    def last_gather(e, a, b):
        mine = 2 * e + core
        for copy in a + b:
            copy.wait_recv()
        ref = fin.at[mine]
        copy = copies.remote(ref, ref, other)
        out = pltpu.make_async_copy(ref, f_out.at[mine], out_sem.at[2 * e])
        out.start()
        return copy, out

    early = first_reduce(0)
    late = first_reduce(1)

    own_rows = pl.ds(pl.multiple_of(head * COLS, COLS), COLS)
    it_copies = []
    for d in range(1, SHARDS):
        rows = pl.ds(pl.multiple_of(at_head(d) * COLS, COLS), COLS)
        it_send[d] = mm_nt(grads[...], wqkv[rows, :]).astype(BF)
        it_copies.append(copies.remote(it_send.at[d], it_recv.at[d], head_dev(d)))

    early = second_reduce(0, *early)
    late = second_reduce(1, *late)
    early = first_gather(0, *early)
    late = first_gather(1, *late)

    total = mm_nt(grads[...], wqkv[own_rows, :])
    for copy in it_copies:
        copy.wait_recv()
    for d in range(1, SHARDS):
        total = total + it_recv[d].astype(F32)
    ig[...] = total.astype(BF)
    ig_copy = pltpu.make_async_copy(ig, ig_out, out_sem.at[4])
    ig_copy.start()

    early = second_gather(0, *early)
    late = second_gather(1, *late)
    early_copy, early_out = last_gather(0, *early)
    late_copy, late_out = last_gather(1, *late)
    early_copy.wait_recv()
    early_rest = pltpu.make_async_copy(fin.at[1 - core], f_out.at[1 - core], out_sem.at[1])
    early_rest.start()
    late_copy.wait_recv()
    late_rest = pltpu.make_async_copy(fin.at[3 - core], f_out.at[3 - core], out_sem.at[3])
    late_rest.start()
    for copy in copies.started:
        copy.wait_send()
    for out in (ig_copy, early_out, late_out, early_rest, late_rest):
        out.wait()


N_COPIES = 7 * 3 + 4 + 2 + 2 * 4 * (NZ - 1 + NY - 1) + 2


def body(inputs, out_grad, w_query, w_key, w_value, w_out, live_rows, window_blocks):
    anyspec = pl.BlockSpec(memory_space=pl.ANY)
    smem = pl.BlockSpec(memory_space=pltpu.SMEM)
    half, piece = BLOCK // 2, BLOCK // 8
    vm = pltpu.VMEM
    input_grad, fin = pl.pallas_call(
        kernel,
        out_shape=(
            jax.ShapeDtypeStruct((ROWS, COLS), BF),
            jax.ShapeDtypeStruct((4, SHARDS, BLOCK, COLS), BF),
        ),
        in_specs=[anyspec] * 6 + [smem] * 2,
        out_specs=(anyspec, anyspec),
        scratch_shapes=[
            vm((SHARDS, ROWS, COLS), BF),
            vm((SHARDS, ROWS, COLS), BF),
            vm((SHARDS * COLS, 3 * COLS), BF),
            vm((COLS, SHARDS * COLS), BF),
            vm((3, ROWS + 16, 2 * COLS), BF),
            vm((2, ROWS, COLS), BF),
            vm((2, ROWS, COLS), BF),
            vm((4, BLOCK, REACH * BLOCK), F32),
            vm((ROWS, COLS), BF),
            vm((ROWS, COLS), BF),
            vm((3 * ROWS, 2 * COLS), F32),
            vm((2, ROWS, 2 * COLS), BF),
            vm((2, ROWS, 2 * COLS), BF),
            vm((ROWS, 3 * COLS), BF),
            vm((4, SHARDS, BLOCK, COLS), BF),
            vm((2, SHARDS, BLOCK, COLS), BF),
            vm((2, SHARDS, BLOCK, COLS), BF),
            vm((2, NZ, half, COLS), BF),
            vm((2, NY, SHARDS, piece, COLS), BF),
            vm((2, half, COLS), BF),
            vm((2, SHARDS, piece, COLS), BF),
            vm((2, NY, piece, COLS), BF),
            vm((2, NZ, piece, COLS), BF),
            vm((4, SHARDS, BLOCK, COLS), BF),
            vm((SHARDS, ROWS, COLS), BF),
            vm((SHARDS, ROWS, COLS), BF),
            vm((ROWS, COLS), BF),
            pltpu.SemaphoreType.DMA((6,)),
            pltpu.SemaphoreType.DMA((N_COPIES,)),
            pltpu.SemaphoreType.DMA((N_COPIES,)),
            pltpu.SemaphoreType.DMA((5,)),
        ],
        compiler_params=pltpu.CompilerParams(
            collective_id=0, has_side_effects=True, vmem_limit_bytes=40 * 1024 * 1024
        ),
        cost_estimate=pl.CostEstimate(
            flops=1200000000, bytes_accessed=3000000, transcendentals=400000
        ),
    )(inputs, out_grad, w_query, w_key, w_value, w_out, live_rows, window_blocks)
    width = SHARDS * COLS
    grad_query = fin[0].reshape(width, COLS)
    grad_out = fin[1].transpose(1, 0, 2).reshape(COLS, width)
    grad_key = fin[2].reshape(width, COLS)
    grad_value = fin[3].reshape(width, COLS)
    return (input_grad, grad_query, grad_key, grad_value, grad_out)


def solution(mesh):
    placed = (
        P("nodes", "heads"),
        P("nodes", "heads"),
        P(None, "heads"),
        P(None, "heads"),
        P(None, "heads"),
        P("heads", None),
        P("nodes"),
        P("nodes", None),
    )
    return jax.shard_map(
        body,
        mesh=mesh,
        in_specs=placed,
        out_specs=(
            P("nodes", "heads"),
            P(None, "heads"),
            P(None, "heads"),
            P(None, "heads"),
            P("heads", None),
        ),
        check_vma=False,
    )
```

```python
import functools

import jax
import jax.numpy as jnp
from jax import lax
from jax.experimental import pallas as pl
from jax.experimental.pallas import tpu as pltpu
from jax.sharding import PartitionSpec as P

HEAD_DIM = 64
BLOCK = 128
REACH = 5
ROWS = 256
COLS = 128
SHARDS = 8
NZ = 8
NY = 4
NX = 4
SCALE = HEAD_DIM ** (-0.5)
BF = jnp.bfloat16
F32 = jnp.float32
MESH = pl.DeviceIdType.MESH
NT = (((1,), (1,)), ((), ()))
TN = (((0,), (0,)), ((), ()))


def mm(a, b):
    return jnp.dot(a, b, preferred_element_type=F32)


def mm_nt(a, b):
    return lax.dot_general(a, b, NT, preferred_element_type=F32)


def mm_tn(a, b):
    return lax.dot_general(a, b, TN, preferred_element_type=F32)


class Copies:
    def __init__(self, send, recv):
        self.send, self.recv, self.used, self.started = send, recv, 0, []

    def planned(self, src, dst, device):
        i = self.used
        self.used += 1
        return pltpu.make_async_remote_copy(
            src_ref=src,
            dst_ref=dst,
            send_sem=self.send.at[i],
            recv_sem=self.recv.at[i],
            device_id=device,
            device_id_type=MESH,
        )

    def remote(self, src, dst, device):
        copy = self.planned(src, dst, device)
        copy.start()
        self.started.append(copy)
        return copy


def kernel(
    x_in, g_in, wq_in, wk_in, wv_in, wo_in, live_in, win_in,
    ig_out, f_out,
    xg, gg, xo, go, xt, wqkv, wqkv_t, wo, wo_t, kv, qm, bm, probs, ad, ad_other, late_other,
    dkv_ext, dkv_send, dkv_recv, grads,
    part, ra1, rb1, sa, sb, ra2, rb2, fin, it_send, it_recv, it_pass, it_last, ig,
    local_sem, send_sem, recv_sem, out_sem,
):
    node = lax.axis_index("nodes")
    head = lax.axis_index("heads")
    core = lax.rem(node, 2)
    z = lax.rem(node // 2, NZ)
    y = node // (2 * NZ)
    nodes = 2 * NZ * NY
    xx = head // 2
    yl = lax.rem(head, 2)

    def at_z(d):
        return lax.rem(z + d, NZ)

    def at_y(d):
        return lax.rem(y + d, NY)

    def at_x(d):
        return lax.rem(xx + d, NX)

    left = (lax.rem(node + nodes - 1, nodes), head)
    right = (lax.rem(node + 1, nodes), head)
    other = (node + 1 - 2 * core, head)

    def z_dev(d):
        return ((y * NZ + at_z(d)) * 2 + core, head)

    def y_dev(d):
        return ((at_y(d) * NZ + z) * 2 + core, head)

    def x_dev(d):
        return (node, at_x(d) * 2 + yl)

    mate_head = xx * 2 + 1 - yl
    mate = (node, mate_head)

    partners = [mate]
    partners += [x_dev(d) for d in range(1, NX)]
    partners += [left, right]
    partners += [z_dev(d) for d in range(1, NZ)]
    partners += [y_dev(d) for d in range(1, NY)]
    barrier = pltpu.get_barrier_semaphore()
    for dev in partners:
        pl.semaphore_signal(barrier, inc=1, device_id=dev, device_id_type=MESH)

    loads = [
        pltpu.make_async_copy(x_in, xg.at[head], local_sem.at[0]),
        pltpu.make_async_copy(wq_in, wqkv.at[0], local_sem.at[1]),
        pltpu.make_async_copy(wk_in, wqkv.at[1], local_sem.at[2]),
        pltpu.make_async_copy(wv_in, wqkv.at[2], local_sem.at[3]),
        pltpu.make_async_copy(g_in, gg.at[head], local_sem.at[4]),
        pltpu.make_async_copy(wo_in, wo, local_sem.at[5]),
    ]
    for load in loads:
        load.start()

    pl.semaphore_wait(barrier, len(partners))
    copies = Copies(send_sem, recv_sem)
    x_a = copies.remote(x_in, xg.at[head], mate)
    x_b = {d: copies.remote(x_in, xg.at[head], x_dev(d)) for d in (1, 3, 2)}
    g_a = copies.remote(g_in, gg.at[head], mate)

    live = live_in[0]
    lane_row = lax.broadcasted_iota(jnp.int32, (16, ROWS), 1)
    kv[1, ROWS : ROWS + 16, :] = jnp.where(lane_row < live, 1.0, 0.0).astype(BF)
    for load in loads:
        load.wait()

    x_a.wait_recv()
    x_c = [copies.remote(xg.at[mate_head], xg.at[mate_head], x_dev(d)) for d in (1, 3)]
    g_b = {d: copies.remote(g_in, gg.at[head], x_dev(d)) for d in (1, 3, 2)}
    far = at_x(2) * 2 + yl
    for j in range(3):
        for s in range(SHARDS):
            wqkv_t[s, j * COLS : (j + 1) * COLS, :] = wqkv[j, s * COLS : (s + 1) * COLS, :].T
    x_b[2].wait_recv()
    x_d = copies.remote(xg.at[far], xg.at[far], mate)
    g_a.wait_recv()
    g_c = [copies.remote(gg.at[mate_head], gg.at[mate_head], x_dev(d)) for d in (1, 3)]
    for copy in (x_b[1], x_b[3], x_c[0], x_c[1], x_d):
        copy.wait_recv()

    x_full = jnp.concatenate([xg[s] for s in range(SHARDS)], axis=1)
    kv[1, 0:ROWS, 0:COLS] = mm(x_full, wqkv[1]).astype(BF)
    kv[1, 0:ROWS, COLS:] = mm(x_full, wqkv[2]).astype(BF)
    kv_right = copies.remote(kv.at[1], kv.at[0], right)
    kv_left = copies.remote(kv.at[1], kv.at[2], left)
    x_core = copies.remote(xg, xo, other)

    first = lax.broadcasted_iota(jnp.int32, (ROWS, COLS), 1) < HEAD_DIM
    queries = mm(x_full, wqkv[0])
    qm[0] = jnp.where(first, queries, 0.0).astype(BF)
    qm[1] = jnp.where(first, 0.0, queries).astype(BF)
    g_b[2].wait_recv()
    g_d = copies.remote(gg.at[far], gg.at[far], mate)
    for s in range(SHARDS):
        xt[s, :, 0:ROWS] = xg[s].T
    for s in range(SHARDS):
        wo_t[s * COLS : (s + 1) * COLS, :] = wo[:, s * COLS : (s + 1) * COLS].T

    kv_right.wait_recv()
    kv_left.wait_recv()

    def reach(b, lo):
        return jnp.concatenate(
            [
                kv[e // 2, (e % 2) * BLOCK : (e % 2 + 1) * BLOCK, lo : lo + COLS]
                for e in range(b, b + REACH)
            ],
            axis=0,
        )

    live_ext = jnp.concatenate([kv[i, ROWS : ROWS + 16, :] for i in range(3)], axis=1)
    live_ext = live_ext.astype(F32)[0:1, :]
    first_b = first[0:BLOCK]
    span = REACH * BLOCK
    col = lax.broadcasted_iota(jnp.int32, (BLOCK, span), 1)
    row = lax.broadcasted_iota(jnp.int32, (BLOCK, span), 0)
    diag = col == row + 2 * BLOCK
    for b in range(2):
        rows = slice(b * BLOCK, (b + 1) * BLOCK)
        keys, vals = reach(b, 0), reach(b, COLS)
        block = lax.broadcasted_iota(jnp.int32, (1, span), 1) // BLOCK + (2 * node - 2 + b)
        chosen = (block == win_in[b, 0]) | (block == win_in[b, 1]) | (block == win_in[b, 2])
        usable = jnp.where(chosen, live_ext[:, b * BLOCK : b * BLOCK + span], 0.0)
        allowed = diag | (jnp.broadcast_to(usable, (BLOCK, span)) > 0.5)
        outs = []
        for h in range(2):
            scores = mm_nt(qm[h, rows, :], keys) * SCALE
            expo = jnp.where(allowed, jnp.exp(scores), 0.0)
            prob = expo / jnp.sum(expo, axis=-1, keepdims=True)
            probs[2 * b + h] = prob
            outs.append(mm(prob.astype(BF), vals))
        ad[1, rows, :] = jnp.where(first_b, outs[0], outs[1]).astype(BF)

    early_copy = copies.planned(ad.at[1 - core], ad_other, other)

    @pl.when(core == 0)
    def _():
        early_copy.start()

    x_core.wait_recv()
    for s in range(SHARDS):
        xt[s, :, ROWS:] = xo[s].T

    for copy in (g_b[1], g_b[3], g_c[0], g_c[1], g_d):
        copy.wait_recv()
    g_core = copies.planned(gg, go, other)

    @pl.when(core == 0)
    def _():
        g_core.start()

    g_full = jnp.concatenate([gg[s] for s in range(SHARDS)], axis=1)
    back = mm(g_full, wo_t[...])
    bm[0] = jnp.where(first, back, 0.0).astype(BF)
    bm[1] = jnp.where(first, 0.0, back).astype(BF)

    for b in range(2):
        rows = slice(b * BLOCK, (b + 1) * BLOCK)
        keys, vals = reach(b, 0), reach(b, COLS)
        outs, dk, dv = [], 0.0, 0.0
        for h in range(2):
            prob = probs[2 * b + h]
            dprob = mm_nt(bm[h, rows, :], vals)
            delta = jnp.sum(prob * dprob, axis=-1, keepdims=True)
            dscore = (SCALE * prob * (dprob - delta)).astype(BF)
            outs.append(mm(dscore, keys))
            dk = dk + mm_tn(dscore, qm[h, rows, :])
            dv = dv + mm_tn(prob.astype(BF), bm[h, rows, :])
        ad[0, rows, :] = jnp.where(first_b, outs[0], outs[1]).astype(BF)
        if b == 0:
            dkv_ext[0:span, 0:COLS] = dk
            dkv_ext[0:span, COLS:] = dv
        else:
            dkv_ext[BLOCK:span, 0:COLS] += dk[0 : span - BLOCK]
            dkv_ext[BLOCK:span, COLS:] += dv[0 : span - BLOCK]
            dkv_ext[span:, 0:COLS] = dk[span - BLOCK :]
            dkv_ext[span:, COLS:] = dv[span - BLOCK :]

    dkv_send[0] = dkv_ext[0:ROWS, :].astype(BF)
    dkv_send[1] = dkv_ext[2 * ROWS :, :].astype(BF)
    dkv_left = copies.remote(dkv_send.at[0], dkv_recv.at[0], left)
    dkv_right = copies.remote(dkv_send.at[1], dkv_recv.at[1], right)

    @pl.when(core == 1)
    def _():
        early_copy.start()


    half, piece = BLOCK // 2, BLOCK // 8

    def low(i):
        return pl.ds(pl.multiple_of(i * piece, piece), piece)

    def high(i):
        return pl.ds(pl.multiple_of(half + i * piece, piece), piece)

    def first_reduce(e):
        a = [
            copies.remote(part.at[e, at_z(d), 0:half, :], ra1.at[e, d], z_dev(d))
            for d in range(1, NZ)
        ]
        b = [
            copies.remote(part.at[e, :, high(at_y(d)), :], rb1.at[e, d], y_dev(d))
            for d in range(1, NY)
        ]
        return a, b

    def second_reduce(e, a, b):
        for copy in a:
            copy.wait_recv()
        total = part[e, z, 0:half, :].astype(F32)
        for d in range(1, NZ):
            total = total + ra1[e, d].astype(F32)
        sa[e] = total.astype(BF)
        a = [copies.remote(sa.at[e, low(at_y(d)), :], ra2.at[e, d], y_dev(d)) for d in range(1, NY)]
        for copy in b:
            copy.wait_recv()
        total = part[e, :, high(y), :].astype(F32)
        for d in range(1, NY):
            total = total + rb1[e, d].astype(F32)
        sb[e] = total.astype(BF)
        b = [copies.remote(sb.at[e, at_z(d)], rb2.at[e, d], z_dev(d)) for d in range(1, NZ)]
        return a, b

    def first_gather(e, a, b):
        mine = 2 * e + core
        for copy in a:
            copy.wait_recv()
        total = sa[e, low(y), :].astype(F32)
        for d in range(1, NY):
            total = total + ra2[e, d].astype(F32)
        fin[e, z, low(y), :] = total.astype(BF)
        ref = fin.at[e, z, low(y), :]
        a = [copies.remote(ref, ref, y_dev(d)) for d in range(1, NY)]
        for copy in b:
            copy.wait_recv()
        total = sb[e, z].astype(F32)
        for d in range(1, NZ):
            total = total + rb2[e, d].astype(F32)
        fin[e, z, high(y), :] = total.astype(BF)
        ref = fin.at[e, z, high(y), :]
        b = [copies.remote(ref, ref, z_dev(d)) for d in range(1, NZ)]
        return a, b

    def second_gather(e, a, b):
        for copy in a:
            copy.wait_recv()
        ref = fin.at[e, z, 0:half, :]
        a = [copies.remote(ref, ref, z_dev(d)) for d in range(1, NZ)]
        for copy in b:
            copy.wait_recv()
        ref = fin.at[e, :, high(y), :]
        b = [copies.remote(ref, ref, y_dev(d)) for d in range(1, NY)]
        return a, b

    def last_gather(e, a, b, whole):
        mine = 2 * e + core
        handed = []
        if not whole:
            handed.append(
                copies.remote(fin.at[e, z, 0:half, :], f_out.at[mine, z, 0:half, :], other)
            )
            handed.append(
                copies.remote(fin.at[e, :, high(y), :], f_out.at[mine, :, high(y), :], other)
            )
        for d, copy in zip(range(1, NZ), a):
            copy.wait_recv()
            if not whole:
                at = at_z(NZ - d)
                handed.append(
                    copies.remote(fin.at[e, at, 0:half, :], f_out.at[mine, at, 0:half, :], other)
                )
        for d, copy in zip(range(1, NY), b):
            copy.wait_recv()
            if not whole:
                at = high(at_y(NY - d))
                handed.append(
                    copies.remote(fin.at[e, :, at, :], f_out.at[mine, :, at, :], other)
                )
        if whole:
            handed.append(copies.remote(fin.at[e], f_out.at[mine], other))
        out = pltpu.make_async_copy(fin.at[e], f_out.at[mine], out_sem.at[e])
        out.start()
        return handed, out

    early_copy.wait_recv()

    @pl.when(core == 0)
    def _():
        part[0, :, :, :] = (
            mm(
                xt[...].reshape(SHARDS * COLS, 2 * ROWS),
                jnp.concatenate([ad[0], ad_other[...]], axis=0),
            )
            .astype(BF)
            .reshape(SHARDS, COLS, COLS)
        )

    @pl.when(core == 1)
    def _():
        g_core.wait_recv()
        lhs = jnp.concatenate([ad[1].T, ad_other[...].T], axis=1)
        for s in range(SHARDS):
            part[0, s] = mm(lhs, jnp.concatenate([gg[s], go[s]], axis=0)).astype(BF)

    early = first_reduce(0)
    dkv_left.wait_recv()
    dkv_right.wait_recv()
    dkv = dkv_ext[ROWS : 2 * ROWS, :] + dkv_recv[0].astype(F32) + dkv_recv[1].astype(F32)
    grads[0] = dkv[:, 0:COLS].astype(BF)
    grads[1] = dkv[:, COLS:].astype(BF)
    late_copy = copies.remote(grads.at[1 - core], late_other, other)

    all_grads = jnp.concatenate([ad[0], grads[0], grads[1]], axis=1)
    it_copies = []
    for d in range(1, NX):
        for i in range(2):
            it_send[d, i] = mm(all_grads, wqkv_t[at_x(d) * 2 + i]).astype(BF)
        it_copies.append(copies.remote(it_send.at[d], it_recv.at[d], x_dev(d)))

    late_copy.wait_recv()
    part[1, :, :, :] = (
        mm(
            xt[...].reshape(SHARDS * COLS, 2 * ROWS),
            jnp.concatenate([grads[core], late_other[...]], axis=0),
        )
        .astype(BF)
        .reshape(SHARDS, COLS, COLS)
    )
    late = first_reduce(1)

    it_keep = mm(all_grads, wqkv_t[head])
    it_give = mm(all_grads, wqkv_t[mate_head])

    early = second_reduce(0, *early)
    for copy in it_copies:
        copy.wait_recv()
    for d in range(1, NX):
        it_keep = it_keep + it_recv[d, yl].astype(F32)
        it_give = it_give + it_recv[d, 1 - yl].astype(F32)
    it_pass[...] = it_give.astype(BF)
    it_copy = copies.remote(it_pass, it_last, mate)
    late = second_reduce(1, *late)
    early = first_gather(0, *early)
    late = first_gather(1, *late)

    it_copy.wait_recv()
    ig[...] = (it_keep + it_last[...].astype(F32)).astype(BF)
    ig_copy = pltpu.make_async_copy(ig, ig_out, out_sem.at[2])
    ig_copy.start()

    early = second_gather(0, *early)
    late = second_gather(1, *late)
    early_handed, early_out = last_gather(0, *early, True)
    late_handed, late_out = last_gather(1, *late, False)
    for copy in early_handed + late_handed:
        copy.wait_recv()
    for copy in copies.started:
        copy.wait_send()

    @pl.when(core == 0)
    def _():
        early_copy.wait_send()
        g_core.wait_send()

    @pl.when(core == 1)
    def _():
        early_copy.wait_send()

    for out in (ig_copy, early_out, late_out):
        out.wait()


N_COPIES = 14 + 4 + 4 + 4 + 2 * 4 * (NZ - 1 + NY - 1) + 1 + NZ + NY


def hand_out(ig_in, f_in, ig_out, q_out, k_out, v_out, o_out, sem):
    parts = [(ig_in, ig_out), (f_in.at[0], q_out), (f_in.at[2], k_out), (f_in.at[3], v_out)]
    parts += [(f_in.at[1, s], o_out.at[:, s * COLS : (s + 1) * COLS]) for s in range(SHARDS)]
    copies = [pltpu.make_async_copy(a, b, sem.at[i]) for i, (a, b) in enumerate(parts)]
    for copy in copies:
        copy.start()
    for copy in copies:
        copy.wait()


def body(inputs, out_grad, w_query, w_key, w_value, w_out, live_rows, window_blocks):
    anyspec = pl.BlockSpec(memory_space=pl.ANY)
    smem = pl.BlockSpec(memory_space=pltpu.SMEM)
    half, piece = BLOCK // 2, BLOCK // 8
    vm = pltpu.VMEM
    params = pltpu.CompilerParams(
        collective_id=0, has_side_effects=True, vmem_limit_bytes=62 * 1024 * 1024
    )
    input_grad, fin = pl.pallas_call(
        kernel,
        out_shape=(
            jax.ShapeDtypeStruct((ROWS, COLS), BF),
            jax.ShapeDtypeStruct((4, SHARDS, BLOCK, COLS), BF),
        ),
        in_specs=[anyspec] * 6 + [smem] * 2,
        out_specs=(anyspec, anyspec),
        scratch_shapes=[
            vm((SHARDS, ROWS, COLS), BF),
            vm((SHARDS, ROWS, COLS), BF),
            vm((SHARDS, ROWS, COLS), BF),
            vm((SHARDS, ROWS, COLS), BF),
            vm((SHARDS, COLS, 2 * ROWS), BF),
            vm((3, SHARDS * COLS, COLS), BF),
            vm((SHARDS, 3 * COLS, COLS), BF),
            vm((COLS, SHARDS * COLS), BF),
            vm((SHARDS * COLS, COLS), BF),
            vm((3, ROWS + 16, 2 * COLS), BF),
            vm((2, ROWS, COLS), BF),
            vm((2, ROWS, COLS), BF),
            vm((4, BLOCK, REACH * BLOCK), F32),
            vm((2, ROWS, COLS), BF),
            vm((ROWS, COLS), BF),
            vm((ROWS, COLS), BF),
            vm((3 * ROWS, 2 * COLS), F32),
            vm((2, ROWS, 2 * COLS), BF),
            vm((2, ROWS, 2 * COLS), BF),
            vm((2, ROWS, COLS), BF),
            vm((2, SHARDS, BLOCK, COLS), BF),
            vm((2, NZ, half, COLS), BF),
            vm((2, NY, SHARDS, piece, COLS), BF),
            vm((2, half, COLS), BF),
            vm((2, SHARDS, piece, COLS), BF),
            vm((2, NY, piece, COLS), BF),
            vm((2, NZ, piece, COLS), BF),
            vm((2, SHARDS, BLOCK, COLS), BF),
            vm((NX, 2, ROWS, COLS), BF),
            vm((NX, 2, ROWS, COLS), BF),
            vm((ROWS, COLS), BF),
            vm((ROWS, COLS), BF),
            vm((ROWS, COLS), BF),
            pltpu.SemaphoreType.DMA((6,)),
            pltpu.SemaphoreType.DMA((N_COPIES,)),
            pltpu.SemaphoreType.DMA((N_COPIES,)),
            pltpu.SemaphoreType.DMA((3,)),
        ],
        compiler_params=params,
        cost_estimate=pl.CostEstimate(
            flops=1200000000, bytes_accessed=3000000, transcendentals=400000
        ),
    )(inputs, out_grad, w_query, w_key, w_value, w_out, live_rows, window_blocks)
    width = SHARDS * COLS
    cols = jax.ShapeDtypeStruct((SHARDS, COLS, COLS), BF)
    input_grad, grad_query, grad_key, grad_value, grad_out = pl.pallas_call(
        hand_out,
        out_shape=(
            jax.ShapeDtypeStruct((ROWS, COLS), BF),
            cols,
            cols,
            cols,
            jax.ShapeDtypeStruct((COLS, width), BF),
        ),
        in_specs=[anyspec] * 2,
        out_specs=[anyspec] * 5,
        scratch_shapes=[pltpu.SemaphoreType.DMA((4 + SHARDS,))],
        cost_estimate=pl.CostEstimate(flops=0, bytes_accessed=2200000, transcendentals=0),
    )(input_grad, fin)
    return (
        input_grad,
        grad_query.reshape(width, COLS),
        grad_key.reshape(width, COLS),
        grad_value.reshape(width, COLS),
        grad_out,
    )


def solution(mesh):
    placed = (
        P("nodes", "heads"),
        P("nodes", "heads"),
        P(None, "heads"),
        P(None, "heads"),
        P(None, "heads"),
        P("heads", None),
        P("nodes"),
        P("nodes", None),
    )
    return jax.shard_map(
        body,
        mesh=mesh,
        in_specs=placed,
        out_specs=(
            P("nodes", "heads"),
            P(None, "heads"),
            P(None, "heads"),
            P(None, "heads"),
            P("heads", None),
        ),
        check_vma=False,
    )
```

```python
import functools

import jax
import jax.numpy as jnp
from jax import lax
from jax.experimental import pallas as pl
from jax.experimental.pallas import tpu as pltpu
from jax.sharding import PartitionSpec as P

HEAD_DIM = 64
BLOCK = 128
ROWS = 256
COLS = 128
SHARDS = 8
NZ = 8
NY = 4
NX = 4
Z_ORDER = (4, 3, 5, 2, 6, 1, 7)
Y_ORDER = (2, 1, 3)
X_ORDER = (2, 1, 3)
TOP = 80
SCALE = HEAD_DIM ** (-0.5)
BF = jnp.bfloat16
F32 = jnp.float32
MESH = pl.DeviceIdType.MESH
NT = (((1,), (1,)), ((), ()))
TN = (((0,), (0,)), ((), ()))


def mm(a, b):
    return jnp.dot(a, b, preferred_element_type=F32)


def mm_nt(a, b):
    return lax.dot_general(a, b, NT, preferred_element_type=F32)


def mm_tn(a, b):
    return lax.dot_general(a, b, TN, preferred_element_type=F32)


class Copies:
    def __init__(self, send, recv):
        self.send, self.recv, self.used, self.started = send, recv, 0, []

    def planned(self, src, dst, device):
        i = self.used
        self.used += 1
        return pltpu.make_async_remote_copy(
            src_ref=src,
            dst_ref=dst,
            send_sem=self.send.at[i],
            recv_sem=self.recv.at[i],
            device_id=device,
            device_id_type=MESH,
        )

    def remote(self, src, dst, device):
        copy = self.planned(src, dst, device)
        copy.start()
        self.started.append(copy)
        return copy


def kernel(
    x_in, g_in, wq_in, wk_in, wv_in, wo_in, live_in, win_in,
    ig_out, f_out,
    xg, gg, xo, go, xt, wq, wkv, w_t, wo, wo_t, kv, qs, bs, expo, dprob, ad, ad_other, late_other,
    dkv_own, dkv_send, dkv_recv, grads,
    part, ra1, rb1, ra2, rb2, fin, it_send, it_recv, it_pass, it_last, ig,
    local_sem, send_sem, recv_sem, out_sem,
):
    node = lax.axis_index("nodes")
    head = lax.axis_index("heads")
    core = lax.rem(node, 2)
    z = lax.rem(node // 2, NZ)
    y = node // (2 * NZ)
    nodes = 2 * NZ * NY
    xx = head // 2
    yl = lax.rem(head, 2)

    def at_z(d):
        return lax.rem(z + d, NZ)

    def at_y(d):
        return lax.rem(y + d, NY)

    def at_x(d):
        return lax.rem(xx + d, NX)

    left = (lax.rem(node + nodes - 1, nodes), head)
    right = (lax.rem(node + 1, nodes), head)
    other = (node + 1 - 2 * core, head)

    def z_dev(d):
        return ((y * NZ + at_z(d)) * 2 + core, head)

    def y_dev(d):
        return ((at_y(d) * NZ + z) * 2 + core, head)

    def x_dev(d):
        return (node, at_x(d) * 2 + yl)

    mate_head = xx * 2 + 1 - yl
    mate = (node, mate_head)

    partners = [z_dev(d) for d in Z_ORDER] + [y_dev(d) for d in Y_ORDER]
    partners += [x_dev(d) for d in X_ORDER] + [mate, left, right]
    barrier = pltpu.get_barrier_semaphore()
    for dev in partners:
        pl.semaphore_signal(barrier, inc=1, device_id=dev, device_id_type=MESH)

    loads = [
        pltpu.make_async_copy(x_in, xg.at[head], local_sem.at[0]),
        pltpu.make_async_copy(wk_in, wkv.at[:, 0:COLS], local_sem.at[1]),
        pltpu.make_async_copy(wv_in, wkv.at[:, COLS:], local_sem.at[2]),
        pltpu.make_async_copy(wq_in, wq, local_sem.at[3]),
        pltpu.make_async_copy(g_in, gg.at[head], local_sem.at[4]),
        pltpu.make_async_copy(wo_in, wo, local_sem.at[5]),
    ]
    for load in loads:
        load.start()
    live = live_in[0]
    lane_row = lax.broadcasted_iota(jnp.int32, (16, ROWS), 1)
    kv[1, ROWS : ROWS + 16, :] = jnp.where(lane_row < live, 1.0, 0.0).astype(BF)

    pl.semaphore_wait(barrier, len(partners))
    copies = Copies(send_sem, recv_sem)
    far = at_x(2) * 2 + yl
    x_b = {2: copies.remote(x_in, xg.at[head], x_dev(2))}
    x_a = copies.remote(x_in, xg.at[head], mate)
    for d in (1, 3):
        x_b[d] = copies.remote(x_in, xg.at[head], x_dev(d))
    g_a = copies.remote(g_in, gg.at[head], mate)
    for load in loads:
        load.wait()

    x_a.wait_recv()
    x_c = [copies.remote(xg.at[mate_head], xg.at[mate_head], x_dev(d)) for d in (1, 3)]
    x_b[2].wait_recv()
    x_d = copies.remote(xg.at[far], xg.at[far], mate)
    g_b = {d: copies.remote(g_in, gg.at[head], x_dev(d)) for d in X_ORDER}
    g_a.wait_recv()
    g_c = [copies.remote(gg.at[mate_head], gg.at[mate_head], x_dev(d)) for d in (1, 3)]
    for s in range(SHARDS):
        rows, cols = slice(s * COLS, (s + 1) * COLS), slice((s % 2) * COLS, (s % 2 + 1) * COLS)
        w_t[s // 2, 0:COLS, cols] = wq[rows, :].T
        w_t[s // 2, COLS:, cols] = wkv[rows, :].T
    for copy in (x_b[1], x_b[3], x_c[0], x_c[1], x_d):
        copy.wait_recv()

    x_full = jnp.concatenate([xg[s] for s in range(SHARDS)], axis=1)
    kv[1, 0:ROWS, :] = mm(x_full, wkv[...]).astype(BF)
    kv_right = copies.remote(kv.at[1], kv.at[0], right)
    kv_left = copies.remote(kv.at[1], kv.at[2], left)
    x_core = copies.remote(xg, xo, other)
    g_b[2].wait_recv()
    g_d = copies.remote(gg.at[far], gg.at[far], mate)

    first = lax.broadcasted_iota(jnp.int32, (ROWS, COLS), 1) < HEAD_DIM
    queries = mm(x_full, wq[...])
    qs[0:ROWS, :] = jnp.where(first, queries, 0.0).astype(BF)
    qs[ROWS:, :] = jnp.where(first, 0.0, queries).astype(BF)

    col = lax.broadcasted_iota(jnp.int32, (ROWS, ROWS), 1)
    row = lax.broadcasted_iota(jnp.int32, (ROWS, ROWS), 0)
    col_block = lax.broadcasted_iota(jnp.int32, (1, ROWS), 1) // BLOCK

    def exponents(i):
        live_row = kv[i, ROWS : ROWS + 16, :].astype(F32)[0:1, :]
        block = col_block + 2 * (node - 1 + i)
        usable = []
        for b in range(2):
            chosen = (block == win_in[b, 0]) | (block == win_in[b, 1]) | (block == win_in[b, 2])
            usable.append(jnp.broadcast_to(jnp.where(chosen, live_row, 0.0), (BLOCK, ROWS)))
        allowed = jnp.concatenate(usable, axis=0) > 0.5
        if i == 1:
            allowed = allowed | (col == row)
        sums = []
        for h in range(2):
            rows = slice(h * ROWS, (h + 1) * ROWS)
            scores = mm_nt(qs[rows, :], kv[i, 0:ROWS, 0:COLS]) * SCALE
            value = jnp.where(allowed, jnp.exp(scores), 0.0)
            expo[i, rows, :] = value
            sums.append(jnp.sum(value, axis=-1, keepdims=True))
        return jnp.concatenate(sums, axis=0)

    total = exponents(1)
    for s in range(SHARDS):
        wo_t[s * COLS : (s + 1) * COLS, :] = wo[:, s * COLS : (s + 1) * COLS].T
    for s in range(SHARDS):
        xt[s, :, 0:ROWS] = xg[s].T
    for copy in (g_b[1], g_b[3], g_c[0], g_c[1], g_d):
        copy.wait_recv()
    g_core = copies.planned(gg, go, other)

    @pl.when(core == 0)
    def _():
        g_core.start()

    g_full = jnp.concatenate([gg[s] for s in range(SHARDS)], axis=1)
    back = mm(g_full, wo_t[...])
    bs[0:ROWS, :] = jnp.where(first, back, 0.0).astype(BF)
    bs[ROWS:, :] = jnp.where(first, 0.0, back).astype(BF)
    dprob[1] = mm_nt(bs[...], kv[1, 0:ROWS, COLS:])
    x_core.wait_recv()
    for s in range(SHARDS):
        xt[s, :, ROWS:] = xo[s].T

    kv_right.wait_recv()
    kv_left.wait_recv()
    total = total + exponents(0) + exponents(2)
    inverse = 1.0 / total
    delta = 0.0
    for i in (1, 0, 2):
        vals = kv[i, 0:ROWS, COLS:]
        prob = expo[i] * inverse
        expo[i] = prob
        if i != 1:
            dprob[i] = mm_nt(bs[...], vals)
        delta = delta + jnp.sum(prob * dprob[i], axis=-1, keepdims=True)

    qs_t, bs_t = qs[...].T, bs[...].T

    def backward(i):
        prob = expo[i]
        dscore = (SCALE * prob * (dprob[i] - delta)).astype(BF)
        low = prob.astype(BF)
        term = mm(dscore, kv[i, 0:ROWS, 0:COLS])
        out = mm(low, kv[i, 0:ROWS, COLS:])
        return mm(qs_t, dscore), mm(bs_t, low), term, out

    dk, dv, dq0, at0 = backward(0)
    dkv_send[0, :, 0:COLS] = dk.astype(BF).T
    dkv_send[0, :, COLS:] = dv.astype(BF).T
    dkv_left = copies.remote(dkv_send.at[0], dkv_recv.at[0], left)
    dk, dv, dq2, at2 = backward(2)
    dkv_send[1, :, 0:COLS] = dk.astype(BF).T
    dkv_send[1, :, COLS:] = dv.astype(BF).T
    dkv_right = copies.remote(dkv_send.at[1], dkv_recv.at[1], right)
    dk, dv, dq1, at1 = backward(1)
    dq = dq0 + dq1 + dq2
    at = at0 + at1 + at2
    ad[0] = jnp.where(first, dq[0:ROWS], dq[ROWS:]).astype(BF)
    ad[1] = jnp.where(first, at[0:ROWS], at[ROWS:]).astype(BF)
    early_copy = copies.remote(ad.at[1 - core], ad_other, other)
    dkv_own[:, 0:COLS] = dk.T
    dkv_own[:, COLS:] = dv.T

    def pair(i):
        return pl.ds(2 * i, 2)

    def reduce_within(e):
        a = [
            copies.remote(part.at[e, at_z(d), 0:TOP, :], ra1.at[e, d], z_dev(d)) for d in Z_ORDER
        ]
        b = [
            copies.remote(part.at[e, pair(at_y(d)), TOP:, :], rb1.at[e, d], y_dev(d))
            for d in Y_ORDER
        ]
        return a, b

    def exchange(e, a, b):
        for copy in b:
            copy.wait_recv()
        total = part[e, pair(y), TOP:, :].astype(F32)
        for d in range(1, NY):
            total = total + rb1[e, d].astype(F32)
        rb2[e, z] = total.astype(BF)
        ref = rb2.at[e, z]
        b = [copies.remote(ref, ref, z_dev(d)) for d in Z_ORDER]
        for copy in a:
            copy.wait_recv()
        total = part[e, z, 0:TOP, :].astype(F32)
        for d in range(1, NZ):
            total = total + ra1[e, d].astype(F32)
        ra2[e, y] = total.astype(BF)
        ref = ra2.at[e, y]
        a = [copies.remote(ref, ref, y_dev(d)) for d in Y_ORDER]
        return a, b

    def gather(e, a, b):
        for copy in a:
            copy.wait_recv()
        total = ra2[e, 0].astype(F32)
        for i in range(1, NY):
            total = total + ra2[e, i].astype(F32)
        fin[e, z, 0:TOP, :] = total.astype(BF)
        ref = fin.at[e, z, 0:TOP, :]
        a = [copies.remote(ref, ref, z_dev(d)) for d in Z_ORDER]
        for copy in b:
            copy.wait_recv()
        total = rb2[e, 0].astype(F32)
        for i in range(1, NZ):
            total = total + rb2[e, i].astype(F32)
        fin[e, pair(y), TOP:, :] = total.astype(BF)
        ref = fin.at[e, pair(y), TOP:, :]
        b = [copies.remote(ref, ref, y_dev(d)) for d in Y_ORDER]
        return a, b

    def hand(e, a, b):
        mine = 2 * e + core

        def top(i):
            return copies.remote(fin.at[e, i, 0:TOP, :], f_out.at[mine, i, 0:TOP, :], other)

        def rest(i):
            return copies.remote(fin.at[e, pair(i), TOP:, :], f_out.at[mine, pair(i), TOP:, :], other)

        handed = [top(z), rest(y)]
        for d, copy in reversed(list(zip(Z_ORDER, a))):
            copy.wait_recv()
            handed.append(top(at_z(NZ - d)))
        for d, copy in reversed(list(zip(Y_ORDER, b))):
            copy.wait_recv()
            handed.append(rest(at_y(NY - d)))
        out = pltpu.make_async_copy(fin.at[e], f_out.at[mine], out_sem.at[e])
        out.start()
        return handed, out

    early_copy.wait_recv()

    @pl.when(core == 0)
    def _():
        part[0, :, :, :] = (
            mm(
                xt[...].reshape(SHARDS * COLS, 2 * ROWS),
                jnp.concatenate([ad[0], ad_other[...]], axis=0),
            )
            .astype(BF)
            .reshape(SHARDS, COLS, COLS)
        )

    @pl.when(core == 1)
    def _():
        g_core.wait_recv()
        lhs = jnp.concatenate([ad[1].T, ad_other[...].T], axis=1)
        for s in range(SHARDS):
            part[0, s] = mm(lhs, jnp.concatenate([gg[s], go[s]], axis=0)).astype(BF)

    early = reduce_within(0)
    dkv_left.wait_recv()
    dkv_right.wait_recv()
    dkv = dkv_own[...] + dkv_recv[0].astype(F32) + dkv_recv[1].astype(F32)
    grads[0] = dkv[:, 0:COLS].astype(BF)
    grads[1] = dkv[:, COLS:].astype(BF)
    late_copy = copies.remote(grads.at[1 - core], late_other, other)

    all_grads = jnp.concatenate([ad[0], grads[0], grads[1]], axis=1)
    it_copies = []
    for d in X_ORDER:
        terms = mm(all_grads, w_t[at_x(d)]).astype(BF)
        it_send[d, 0] = terms[:, 0:COLS]
        it_send[d, 1] = terms[:, COLS:]
        it_copies.append(copies.remote(it_send.at[d], it_recv.at[d], x_dev(d)))

    late_copy.wait_recv()
    part[1, :, :, :] = (
        mm(
            xt[...].reshape(SHARDS * COLS, 2 * ROWS),
            jnp.concatenate([grads[core], late_other[...]], axis=0),
        )
        .astype(BF)
        .reshape(SHARDS, COLS, COLS)
    )
    late = reduce_within(1)
    early = exchange(0, *early)
    late = exchange(1, *late)
    early = gather(0, *early)

    it_own = mm(all_grads, w_t[xx])
    low, high = it_own[:, 0:COLS], it_own[:, COLS:]
    for copy in it_copies:
        copy.wait_recv()
    for d in range(1, NX):
        low = low + it_recv[d, 0].astype(F32)
        high = high + it_recv[d, 1].astype(F32)
    is_low = jnp.full((ROWS, COLS), yl, jnp.int32) == 0
    it_pass[...] = jnp.where(is_low, high, low).astype(BF)
    it_copy = copies.remote(it_pass, it_last, mate)

    late = gather(1, *late)
    it_copy.wait_recv()
    ig[...] = (jnp.where(is_low, low, high) + it_last[...].astype(F32)).astype(BF)
    ig_copy = pltpu.make_async_copy(ig, ig_out, out_sem.at[2])
    ig_copy.start()

    early_handed, early_out = hand(0, *early)
    late_handed, late_out = hand(1, *late)
    for copy in early_handed + late_handed:
        copy.wait_recv()
    for copy in copies.started:
        copy.wait_send()

    @pl.when(core == 0)
    def _():
        g_core.wait_send()

    for out in (ig_copy, early_out, late_out):
        out.wait()


N_COPIES = 14 + 4 + 4 + 4 + 2 * 3 * (NZ - 1 + NY - 1) + 2 * (NZ + NY)


def hand_out(ig_in, f_in, ig_out, q_out, k_out, v_out, o_out, ig, fin, sem):
    loads = [pltpu.make_async_copy(f_in.at[i], fin.at[i], sem.at[i]) for i in range(4)]
    loads.append(pltpu.make_async_copy(ig_in, ig, sem.at[4]))
    for load in loads:
        load.start()
    stores = [[(fin.at[0], q_out)]]
    stores.append([(fin.at[1, s], o_out.at[:, s * COLS : (s + 1) * COLS]) for s in range(SHARDS)])
    stores += [[(fin.at[2], k_out)], [(fin.at[3], v_out)], [(ig, ig_out)]]
    started = []
    for load, pairs in zip(loads, stores):
        load.wait()
        for src, dst in pairs:
            started.append(pltpu.make_async_copy(src, dst, sem.at[5 + len(started)]))
            started[-1].start()
    for store in started:
        store.wait()


def body(inputs, out_grad, w_query, w_key, w_value, w_out, live_rows, window_blocks):
    anyspec = pl.BlockSpec(memory_space=pl.ANY)
    smem = pl.BlockSpec(memory_space=pltpu.SMEM)
    vm = pltpu.VMEM
    params = pltpu.CompilerParams(
        collective_id=0, has_side_effects=True, vmem_limit_bytes=62 * 1024 * 1024
    )
    input_grad, fin = pl.pallas_call(
        kernel,
        out_shape=(
            jax.ShapeDtypeStruct((ROWS, COLS), BF),
            jax.ShapeDtypeStruct((4, SHARDS, BLOCK, COLS), BF),
        ),
        in_specs=[anyspec] * 6 + [smem] * 2,
        out_specs=(anyspec, anyspec),
        scratch_shapes=[
            vm((SHARDS, ROWS, COLS), BF),
            vm((SHARDS, ROWS, COLS), BF),
            vm((SHARDS, ROWS, COLS), BF),
            vm((SHARDS, ROWS, COLS), BF),
            vm((SHARDS, COLS, 2 * ROWS), BF),
            vm((SHARDS * COLS, COLS), BF),
            vm((SHARDS * COLS, 2 * COLS), BF),
            vm((NX, 3 * COLS, 2 * COLS), BF),
            vm((COLS, SHARDS * COLS), BF),
            vm((SHARDS * COLS, COLS), BF),
            vm((3, ROWS + 16, 2 * COLS), BF),
            vm((2 * ROWS, COLS), BF),
            vm((2 * ROWS, COLS), BF),
            vm((3, 2 * ROWS, ROWS), F32),
            vm((3, 2 * ROWS, ROWS), F32),
            vm((2, ROWS, COLS), BF),
            vm((ROWS, COLS), BF),
            vm((ROWS, COLS), BF),
            vm((ROWS, 2 * COLS), F32),
            vm((2, ROWS, 2 * COLS), BF),
            vm((2, ROWS, 2 * COLS), BF),
            vm((2, ROWS, COLS), BF),
            vm((2, SHARDS, BLOCK, COLS), BF),
            vm((2, NZ, TOP, COLS), BF),
            vm((2, NY, 2, BLOCK - TOP, COLS), BF),
            vm((2, NY, TOP, COLS), BF),
            vm((2, NZ, 2, BLOCK - TOP, COLS), BF),
            vm((2, SHARDS, BLOCK, COLS), BF),
            vm((NX, 2, ROWS, COLS), BF),
            vm((NX, 2, ROWS, COLS), BF),
            vm((ROWS, COLS), BF),
            vm((ROWS, COLS), BF),
            vm((ROWS, COLS), BF),
            pltpu.SemaphoreType.DMA((6,)),
            pltpu.SemaphoreType.DMA((N_COPIES,)),
            pltpu.SemaphoreType.DMA((N_COPIES,)),
            pltpu.SemaphoreType.DMA((3,)),
        ],
        compiler_params=params,
        cost_estimate=pl.CostEstimate(
            flops=1200000000, bytes_accessed=3000000, transcendentals=400000
        ),
    )(inputs, out_grad, w_query, w_key, w_value, w_out, live_rows, window_blocks)
    width = SHARDS * COLS
    cols = jax.ShapeDtypeStruct((SHARDS, COLS, COLS), BF)
    input_grad, grad_query, grad_key, grad_value, grad_out = pl.pallas_call(
        hand_out,
        out_shape=(
            jax.ShapeDtypeStruct((ROWS, COLS), BF),
            cols,
            cols,
            cols,
            jax.ShapeDtypeStruct((COLS, width), BF),
        ),
        in_specs=[anyspec] * 2,
        out_specs=[anyspec] * 5,
        scratch_shapes=[
            vm((ROWS, COLS), BF),
            vm((4, SHARDS, BLOCK, COLS), BF),
            pltpu.SemaphoreType.DMA((9 + SHARDS,)),
        ],
        compiler_params=pltpu.CompilerParams(vmem_limit_bytes=62 * 1024 * 1024),
        cost_estimate=pl.CostEstimate(flops=0, bytes_accessed=2200000, transcendentals=0),
    )(input_grad, fin)
    return (
        input_grad,
        grad_query.reshape(width, COLS),
        grad_key.reshape(width, COLS),
        grad_value.reshape(width, COLS),
        grad_out,
    )


def solution(mesh):
    placed = (
        P("nodes", "heads"),
        P("nodes", "heads"),
        P(None, "heads"),
        P(None, "heads"),
        P(None, "heads"),
        P("heads", None),
        P("nodes"),
        P("nodes", None),
    )
    return jax.shard_map(
        body,
        mesh=mesh,
        in_specs=placed,
        out_specs=(
            P("nodes", "heads"),
            P(None, "heads"),
            P(None, "heads"),
            P(None, "heads"),
            P("heads", None),
        ),
        check_vma=False,
    )
```

```python
import math

import jax
import jax.numpy as jnp
from jax import lax
from jax.experimental import pallas as pl
from jax.experimental.pallas import tpu as pltpu
from jax.sharding import PartitionSpec as P

HEAD_DIM = 64
BLOCK = 128
ROWS = 256
COLS = 128
SHARDS = 8
NZ = 8
NY = 4
NX = 4
Z_ORDER = (4, 3, 5, 2, 6, 1, 7)
Y_ORDER = (2, 1, 3)
X_ORDER = (2, 1, 3)
TOPS = (64, 80)
PIECE = 16
SCALE = HEAD_DIM ** (-0.5)
BF = jnp.bfloat16
F32 = jnp.float32
MESH = pl.DeviceIdType.MESH
NT = (((1,), (1,)), ((), ()))
TN = (((0,), (0,)), ((), ()))


def mm(a, b):
    return jnp.dot(a, b, preferred_element_type=F32)


def mm_nt(a, b):
    return lax.dot_general(a, b, NT, preferred_element_type=F32)


def mm_tn(a, b):
    return lax.dot_general(a, b, TN, preferred_element_type=F32)


def rows_of(ref):
    return math.prod(ref.shape) // COLS


class Group:
    def __init__(self, copies, index):
        self.copies, self.index, self.rows = copies, index, 0

    def send(self, src, dst, device):
        self.rows += rows_of(src)
        pltpu.make_async_remote_copy(
            src_ref=src,
            dst_ref=dst,
            send_sem=self.copies.pool(rows_of(src)),
            recv_sem=self.copies.recv.at[self.index],
            device_id=device,
            device_id_type=MESH,
        ).start()
        return self

    def wait(self):
        ref = self.copies.tally.at[0 : self.rows, :]
        pltpu.make_async_copy(ref, ref, self.copies.recv.at[self.index]).wait()


class Copies:
    def __init__(self, send, recv, tally):
        self.send, self.recv, self.tally = send, recv, tally
        self.groups, self.pools = 0, [0]

    def group(self):
        self.groups += 1
        return Group(self, self.groups - 1)

    def pool(self, rows):
        if self.pools[-1] + rows > POOL_ROWS:
            self.pools.append(0)
        self.pools[-1] += rows
        return self.send.at[len(self.pools) - 1]

    def finish(self):
        for i, rows in enumerate(self.pools):
            ref = self.tally.at[0:rows, :]
            pltpu.make_async_copy(ref, ref, self.send.at[i]).wait()


def kernel(
    x_in, g_in, wq_in, wk_in, wv_in, wo_in, live_in, win_in,
    ig_out, f_out,
    xg, gg, xo, go, xt, wq, wkv, w_t, wo, wo_t, kv, qs, bs, expo, ad, ad_other, late_other,
    dkv_own, dkv_send, dkv_recv, grads,
    part, ra1, rb1, ra2, rb2, fin, it_send, it_recv, it_pass, it_last, ig,
    ea1, eb1, ea2, es2, eb2, tally, live_s, win_s,
    local_sem, send_sem, recv_sem, pair_sem, out_sem,
):
    node = lax.axis_index("nodes")
    head = lax.axis_index("heads")
    core = lax.rem(node, 2)
    z = lax.rem(node // 2, NZ)
    y = node // (2 * NZ)
    nodes = 2 * NZ * NY
    xx = head // 2
    yl = lax.rem(head, 2)

    def at_z(d):
        return lax.rem(z + d, NZ)

    def at_y(d):
        return lax.rem(y + d, NY)

    def at_x(d):
        return lax.rem(xx + d, NX)

    left = (lax.rem(node + nodes - 1, nodes), head)
    right = (lax.rem(node + 1, nodes), head)
    other = (node + 1 - 2 * core, head)

    def z_dev(d):
        return ((y * NZ + at_z(d)) * 2 + core, head)

    def y_dev(d):
        return ((at_y(d) * NZ + z) * 2 + core, head)

    def x_dev(d):
        return (node, at_x(d) * 2 + yl)

    mate_head = xx * 2 + 1 - yl
    mate = (node, mate_head)

    partners = [z_dev(d) for d in Z_ORDER] + [y_dev(d) for d in Y_ORDER]
    partners += [x_dev(d) for d in X_ORDER] + [mate, left, right]
    barrier = pltpu.get_barrier_semaphore()
    for dev in partners:
        pl.semaphore_signal(barrier, inc=1, device_id=dev, device_id_type=MESH)

    scalars = [
        pltpu.make_async_copy(live_in, live_s, local_sem.at[0]),
        pltpu.make_async_copy(win_in, win_s, local_sem.at[1]),
    ]
    loads = [
        pltpu.make_async_copy(x_in, xg.at[head], local_sem.at[2]),
        pltpu.make_async_copy(g_in, gg.at[head], local_sem.at[2]),
        pltpu.make_async_copy(wk_in, wkv.at[:, 0:COLS], local_sem.at[3]),
        pltpu.make_async_copy(wv_in, wkv.at[:, COLS:], local_sem.at[3]),
        pltpu.make_async_copy(wq_in, wq, local_sem.at[4]),
        pltpu.make_async_copy(wo_in, wo, local_sem.at[4]),
    ]
    for load in scalars + loads:
        load.start()

    pl.semaphore_wait(barrier, len(partners))
    copies = Copies(send_sem, recv_sem, tally)
    far = at_x(2) * 2 + yl
    x_far, x_mate, x_rest = copies.group(), copies.group(), copies.group()
    x_far.send(x_in, xg.at[head], x_dev(2))
    x_mate.send(x_in, xg.at[head], mate)
    for d in (1, 3):
        x_rest.send(x_in, xg.at[head], x_dev(d))
    g_far, g_mate, g_rest = copies.group(), copies.group(), copies.group()
    g_mate.send(g_in, gg.at[head], mate)
    for load in scalars:
        load.wait()
    live = live_s[0]
    lane_row = lax.broadcasted_iota(jnp.int32, (16, ROWS), 1)
    kv[1, ROWS : ROWS + 16, :] = jnp.where(lane_row < live, 1.0, 0.0).astype(BF)
    pltpu.make_async_copy(xg.at[0:2], xg.at[0:2], local_sem.at[2]).wait()
    pltpu.make_async_copy(wkv, wkv, local_sem.at[3]).wait()
    pltpu.make_async_copy(wkv, wkv, local_sem.at[4]).wait()

    x_mate.wait()
    for d in (1, 3):
        x_rest.send(xg.at[mate_head], xg.at[mate_head], x_dev(d))
    x_far.wait()
    x_rest.send(xg.at[far], xg.at[far], mate)
    g_far.send(g_in, gg.at[head], x_dev(2))
    for d in (1, 3):
        g_rest.send(g_in, gg.at[head], x_dev(d))
    g_mate.wait()
    for d in (1, 3):
        g_rest.send(gg.at[mate_head], gg.at[mate_head], x_dev(d))
    for s in range(SHARDS):
        rows, cols = slice(s * COLS, (s + 1) * COLS), slice((s % 2) * COLS, (s % 2 + 1) * COLS)
        w_t[s // 2, 0:COLS, cols] = wq[rows, :].T
        w_t[s // 2, COLS:, cols] = wkv[rows, :].T
    x_rest.wait()

    x_full = jnp.concatenate([xg[s] for s in range(SHARDS)], axis=1)
    kv[1, 0:ROWS, :] = mm(x_full, wkv[...]).astype(BF)
    kv_halo = copies.group()
    kv_halo.send(kv.at[1], kv.at[0], right)
    kv_halo.send(kv.at[1], kv.at[2], left)
    x_core = copies.group().send(xg, xo, other)
    g_far.wait()
    g_rest.send(gg.at[far], gg.at[far], mate)

    first = lax.broadcasted_iota(jnp.int32, (ROWS, COLS), 1) < HEAD_DIM
    queries = mm(x_full, wq[...])
    qs[0:ROWS, :] = jnp.where(first, queries, 0.0).astype(BF)
    qs[ROWS:, :] = jnp.where(first, 0.0, queries).astype(BF)

    col = lax.broadcasted_iota(jnp.int32, (ROWS, ROWS), 1)
    row = lax.broadcasted_iota(jnp.int32, (ROWS, ROWS), 0)
    col_block = lax.broadcasted_iota(jnp.int32, (1, ROWS), 1) // BLOCK

    def exponents(i):
        live_row = kv[i, ROWS : ROWS + 16, :].astype(F32)[0:1, :]
        block = col_block + 2 * (node - 1 + i)
        usable = []
        for b in range(2):
            chosen = (block == win_s[b, 0]) | (block == win_s[b, 1]) | (block == win_s[b, 2])
            usable.append(jnp.broadcast_to(jnp.where(chosen, live_row, 0.0), (BLOCK, ROWS)))
        allowed = jnp.concatenate(usable, axis=0) > 0.5
        if i == 1:
            allowed = allowed | (col == row)
        sums = []
        for h in range(2):
            rows = slice(h * ROWS, (h + 1) * ROWS)
            scores = mm_nt(qs[rows, :], kv[i, 0:ROWS, 0:COLS]) * SCALE
            value = jnp.where(allowed, jnp.exp(scores), 0.0)
            expo[i, rows, :] = value
            sums.append(jnp.sum(value, axis=-1, keepdims=True))
        return jnp.concatenate(sums, axis=0)

    total = exponents(1)
    qs_t = qs[...].T
    for s in range(SHARDS):
        wo_t[s * COLS : (s + 1) * COLS, :] = wo[:, s * COLS : (s + 1) * COLS].T
    for s in range(SHARDS):
        xt[s, :, 0:ROWS] = xg[s].T
    g_rest.wait()
    g_core = pltpu.make_async_remote_copy(
        src_ref=gg,
        dst_ref=go,
        send_sem=pair_sem.at[0],
        recv_sem=pair_sem.at[1],
        device_id=other,
        device_id_type=MESH,
    )

    @pl.when(core == 0)
    def _():
        g_core.start()

    g_full = jnp.concatenate([gg[s] for s in range(SHARDS)], axis=1)
    back = mm(g_full, wo_t[...])
    bs[0:ROWS, :] = jnp.where(first, back, 0.0).astype(BF)
    bs[ROWS:, :] = jnp.where(first, 0.0, back).astype(BF)
    bs_t = bs[...].T
    x_core.wait()
    for s in range(SHARDS):
        xt[s, :, ROWS:] = xo[s].T

    def keys(i):
        return kv[i, 0:ROWS, 0:COLS]

    def vals(i):
        return kv[i, 0:ROWS, COLS:]

    dprob = {1: mm_nt(bs[...], vals(1))}
    kv_halo.wait()
    total = total + exponents(0) + exponents(2)
    inverse = 1.0 / total
    prob, low = {}, {}
    dkv_halo = copies.group()
    for j, i, dev in ((0, 0, left), (1, 2, right)):
        prob[i] = expo[i] * inverse
        low[i] = prob[i].astype(BF)
        dkv_send[j, 1] = mm(bs_t, low[i]).astype(BF).T
        dkv_halo.send(dkv_send.at[j, 1], dkv_recv.at[j, 1], dev)
    prob[1] = expo[1] * inverse
    dprob[0] = mm_nt(bs[...], vals(0))
    dprob[2] = mm_nt(bs[...], vals(2))
    delta = 0.0
    for i in range(3):
        delta = delta + jnp.sum(prob[i] * dprob[i], axis=-1, keepdims=True)
    dscore = {}
    for j, i, dev in ((0, 0, left), (1, 2, right)):
        dscore[i] = (SCALE * prob[i] * (dprob[i] - delta)).astype(BF)
        dkv_send[j, 0] = mm(qs_t, dscore[i]).astype(BF).T
        dkv_halo.send(dkv_send.at[j, 0], dkv_recv.at[j, 0], dev)

    early_copy = pltpu.make_async_remote_copy(
        src_ref=ad.at[1 - core],
        dst_ref=ad_other,
        send_sem=pair_sem.at[2],
        recv_sem=pair_sem.at[3],
        device_id=other,
        device_id_type=MESH,
    )
    low[1] = prob[1].astype(BF)
    at = mm(low[0], vals(0)) + mm(low[1], vals(1)) + mm(low[2], vals(2))
    ad[1] = jnp.where(first, at[0:ROWS], at[ROWS:]).astype(BF)

    @pl.when(core == 0)
    def _():
        early_copy.start()

    dscore[1] = (SCALE * prob[1] * (dprob[1] - delta)).astype(BF)
    dq = mm(dscore[0], keys(0)) + mm(dscore[1], keys(1)) + mm(dscore[2], keys(2))
    ad[0] = jnp.where(first, dq[0:ROWS], dq[ROWS:]).astype(BF)

    @pl.when(core == 1)
    def _():
        early_copy.start()

    dkv_own[0] = mm(qs_t, dscore[1]).T
    dkv_own[1] = mm(bs_t, low[1]).T

    def pair(i):
        return pl.ds(2 * i, 2)

    def to_all(devices, order, src, dst):
        group = copies.group()
        for d in order:
            group.send(src(d), dst(d), devices(d))
        return group

    def reduce_within(e, top, a_in, b_in):
        a = to_all(z_dev, Z_ORDER, lambda d: part.at[e, at_z(d), 0:top, :], lambda d: a_in.at[d])
        b = to_all(
            y_dev, Y_ORDER, lambda d: part.at[e, pair(at_y(d)), top:, :], lambda d: b_in.at[d]
        )
        return a, b

    def added(own, arrived, count):
        total = own.astype(F32)
        for d in range(1, count):
            total = total + arrived[d].astype(F32)
        return total.astype(BF)

    def added_in_order(copies_in, count):
        total = copies_in[0].astype(F32)
        for i in range(1, count):
            total = total + copies_in[i].astype(F32)
        return total.astype(BF)

    def spread(devices, order, ref):
        return to_all(devices, order, lambda d: ref, lambda d: ref)

    def hand(e, a, b):
        mine, top = 2 * e + core, TOPS[e]
        group = copies.group()
        b.wait()
        group.send(fin.at[e, :, top:, :], f_out.at[mine, :, top:, :], other)
        a.wait()
        group.send(fin.at[e, :, 0:top, :], f_out.at[mine, :, 0:top, :], other)
        out = pltpu.make_async_copy(fin.at[e], f_out.at[mine], out_sem.at[e])
        out.start()
        return group, out

    early_copy.wait_recv()

    @pl.when(core == 0)
    def _():
        part[0, :, :, :] = (
            mm(
                xt[...].reshape(SHARDS * COLS, 2 * ROWS),
                jnp.concatenate([ad[0], ad_other[...]], axis=0),
            )
            .astype(BF)
            .reshape(SHARDS, COLS, COLS)
        )

    @pl.when(core == 1)
    def _():
        g_core.wait_recv()
        lhs = jnp.concatenate([ad[1].T, ad_other[...].T], axis=1)
        for s in range(SHARDS):
            part[0, s] = mm(lhs, jnp.concatenate([gg[s], go[s]], axis=0)).astype(BF)

    early_a, early_b = reduce_within(0, TOPS[0], ea1, eb1)
    dkv_halo.wait()
    for i in range(2):
        grads[i] = (dkv_own[i] + dkv_recv[0, i].astype(F32) + dkv_recv[1, i].astype(F32)).astype(BF)
    late_copy = copies.group().send(grads.at[1 - core], late_other, other)

    all_grads = jnp.concatenate([ad[0], grads[0], grads[1]], axis=1)
    it_copies = copies.group()
    for d in X_ORDER:
        terms = mm(all_grads, w_t[at_x(d)]).astype(BF)
        it_send[d, 0] = terms[:, 0:COLS]
        it_send[d, 1] = terms[:, COLS:]
        it_copies.send(it_send.at[d], it_recv.at[d], x_dev(d))

    late_copy.wait()
    part[1, :, :, :] = (
        mm(
            xt[...].reshape(SHARDS * COLS, 2 * ROWS),
            jnp.concatenate([grads[core], late_other[...]], axis=0),
        )
        .astype(BF)
        .reshape(SHARDS, COLS, COLS)
    )
    late_a, late_b = reduce_within(1, TOPS[1], ra1, rb1)

    top = TOPS[0]
    early_a.wait()
    ea2[y] = added(part[0, z, 0:top, :], ea1, NZ)
    early_a = spread(y_dev, Y_ORDER, ea2.at[y])
    early_b.wait()
    es2[...] = added(part[0, pair(y), top:, :], eb1, NY)

    def piece(i):
        return lax.rem(i, 4) * PIECE

    def es2_piece(d):
        i = at_z(d)
        return es2.at[i // 4, pl.ds(pl.multiple_of(piece(i), PIECE), PIECE), :]

    early_b = to_all(z_dev, Z_ORDER, es2_piece, lambda d: eb2.at[d])

    late_b.wait()
    rb2[z] = added(part[1, pair(y), TOPS[1] :, :], rb1, NY)
    late_b = spread(z_dev, Z_ORDER, rb2.at[z])
    late_a.wait()
    ra2[y] = added(part[1, z, 0 : TOPS[1], :], ra1, NZ)
    late_a = spread(y_dev, Y_ORDER, ra2.at[y])

    early_b.wait()
    own_piece = pl.ds(pl.multiple_of(piece(z), PIECE), PIECE)
    place = pl.ds(pl.multiple_of(top + piece(z), PIECE), PIECE)
    fin[0, 2 * y + z // 4, place, :] = added(es2[z // 4, own_piece, :], eb2, NZ)
    early_b = spread(z_dev, Z_ORDER, fin.at[0, 2 * y + z // 4, place, :])
    early_a.wait()
    fin[0, z, 0:top, :] = added_in_order(ea2, NY)
    early_a = spread(z_dev, Z_ORDER, fin.at[0, z, 0:top, :])

    it_own = mm(all_grads, w_t[xx])
    low_half, high_half = it_own[:, 0:COLS], it_own[:, COLS:]
    it_copies.wait()
    for d in range(1, NX):
        low_half = low_half + it_recv[d, 0].astype(F32)
        high_half = high_half + it_recv[d, 1].astype(F32)
    is_low = jnp.full((ROWS, COLS), yl, jnp.int32) == 0
    it_pass[...] = jnp.where(is_low, high_half, low_half).astype(BF)
    it_copy = copies.group().send(it_pass, it_last, mate)

    late_a.wait()
    fin[1, z, 0 : TOPS[1], :] = added_in_order(ra2, NY)
    late_a = spread(z_dev, Z_ORDER, fin.at[1, z, 0 : TOPS[1], :])
    early_b.wait()
    early_b = spread(y_dev, Y_ORDER, fin.at[0, pair(y), top:, :])
    late_b.wait()
    fin[1, pair(y), TOPS[1] :, :] = added_in_order(rb2, NZ)
    late_b = spread(y_dev, Y_ORDER, fin.at[1, pair(y), TOPS[1] :, :])
    it_copy.wait()
    ig[...] = (jnp.where(is_low, low_half, high_half) + it_last[...].astype(F32)).astype(BF)
    ig_copy = pltpu.make_async_copy(ig, ig_out, out_sem.at[2])
    ig_copy.start()

    early_handed, early_out = hand(0, early_a, early_b)
    late_handed, late_out = hand(1, late_a, late_b)
    early_handed.wait()
    late_handed.wait()
    copies.finish()
    early_copy.wait_send()

    @pl.when(core == 0)
    def _():
        g_core.wait_send()

    for out in (ig_copy, early_out, late_out):
        out.wait()


POOL_ROWS = 2560
N_GROUPS = 27
N_POOLS = 7


def hand_out(ig_in, f_in, ig_out, q_out, k_out, v_out, o_out, ig, fin, sem):
    loads = [pltpu.make_async_copy(f_in.at[i], fin.at[i], sem.at[i]) for i in range(4)]
    loads.append(pltpu.make_async_copy(ig_in, ig, sem.at[4]))
    for load in loads:
        load.start()
    stores = [[(fin.at[0], q_out)]]
    stores.append([(fin.at[1, s], o_out.at[:, s * COLS : (s + 1) * COLS]) for s in range(SHARDS)])
    stores += [[(fin.at[2], k_out)], [(fin.at[3], v_out)], [(ig, ig_out)]]
    started = []
    for load, pairs in zip(loads, stores):
        load.wait()
        for src, dst in pairs:
            started.append(pltpu.make_async_copy(src, dst, sem.at[5 + len(started)]))
            started[-1].start()
    for store in started:
        store.wait()


def body(inputs, out_grad, w_query, w_key, w_value, w_out, live_rows, window_blocks):
    anyspec = pl.BlockSpec(memory_space=pl.ANY)
    vm = pltpu.VMEM
    params = pltpu.CompilerParams(
        collective_id=0, has_side_effects=True, vmem_limit_bytes=62 * 1024 * 1024
    )
    input_grad, fin = pl.pallas_call(
        kernel,
        out_shape=(
            jax.ShapeDtypeStruct((ROWS, COLS), BF),
            jax.ShapeDtypeStruct((4, SHARDS, BLOCK, COLS), BF),
        ),
        in_specs=[anyspec] * 8,
        out_specs=(anyspec, anyspec),
        scratch_shapes=[
            vm((SHARDS, ROWS, COLS), BF),
            vm((SHARDS, ROWS, COLS), BF),
            vm((SHARDS, ROWS, COLS), BF),
            vm((SHARDS, ROWS, COLS), BF),
            vm((SHARDS, COLS, 2 * ROWS), BF),
            vm((SHARDS * COLS, COLS), BF),
            vm((SHARDS * COLS, 2 * COLS), BF),
            vm((NX, 3 * COLS, 2 * COLS), BF),
            vm((COLS, SHARDS * COLS), BF),
            vm((SHARDS * COLS, COLS), BF),
            vm((3, ROWS + 16, 2 * COLS), BF),
            vm((2 * ROWS, COLS), BF),
            vm((2 * ROWS, COLS), BF),
            vm((3, 2 * ROWS, ROWS), F32),
            vm((2, ROWS, COLS), BF),
            vm((ROWS, COLS), BF),
            vm((ROWS, COLS), BF),
            vm((2, ROWS, COLS), F32),
            vm((2, 2, ROWS, COLS), BF),
            vm((2, 2, ROWS, COLS), BF),
            vm((2, ROWS, COLS), BF),
            vm((2, SHARDS, BLOCK, COLS), BF),
            vm((NZ, TOPS[1], COLS), BF),
            vm((NY, 2, BLOCK - TOPS[1], COLS), BF),
            vm((NY, TOPS[1], COLS), BF),
            vm((NZ, 2, BLOCK - TOPS[1], COLS), BF),
            vm((2, SHARDS, BLOCK, COLS), BF),
            vm((NX, 2, ROWS, COLS), BF),
            vm((NX, 2, ROWS, COLS), BF),
            vm((ROWS, COLS), BF),
            vm((ROWS, COLS), BF),
            vm((ROWS, COLS), BF),
            vm((NZ, TOPS[0], COLS), BF),
            vm((NY, 2, BLOCK - TOPS[0], COLS), BF),
            vm((NY, TOPS[0], COLS), BF),
            vm((2, BLOCK - TOPS[0], COLS), BF),
            vm((NZ, PIECE, COLS), BF),
            vm((POOL_ROWS, COLS), BF),
            pltpu.SMEM((1,), jnp.int32),
            pltpu.SMEM((2, 3), jnp.int32),
            pltpu.SemaphoreType.DMA((5,)),
            pltpu.SemaphoreType.DMA((N_POOLS,)),
            pltpu.SemaphoreType.DMA((N_GROUPS,)),
            pltpu.SemaphoreType.DMA((4,)),
            pltpu.SemaphoreType.DMA((3,)),
        ],
        compiler_params=params,
        cost_estimate=pl.CostEstimate(
            flops=1200000000, bytes_accessed=3000000, transcendentals=400000
        ),
    )(inputs, out_grad, w_query, w_key, w_value, w_out, live_rows, window_blocks)
    width = SHARDS * COLS
    cols = jax.ShapeDtypeStruct((SHARDS, COLS, COLS), BF)
    input_grad, grad_query, grad_key, grad_value, grad_out = pl.pallas_call(
        hand_out,
        out_shape=(
            jax.ShapeDtypeStruct((ROWS, COLS), BF),
            cols,
            cols,
            cols,
            jax.ShapeDtypeStruct((COLS, width), BF),
        ),
        in_specs=[anyspec] * 2,
        out_specs=[anyspec] * 5,
        scratch_shapes=[
            vm((ROWS, COLS), BF),
            vm((4, SHARDS, BLOCK, COLS), BF),
            pltpu.SemaphoreType.DMA((9 + SHARDS,)),
        ],
        compiler_params=pltpu.CompilerParams(vmem_limit_bytes=62 * 1024 * 1024),
        cost_estimate=pl.CostEstimate(flops=0, bytes_accessed=2200000, transcendentals=0),
    )(input_grad, fin)
    return (
        input_grad,
        grad_query.reshape(width, COLS),
        grad_key.reshape(width, COLS),
        grad_value.reshape(width, COLS),
        grad_out,
    )


def solution(mesh):
    placed = (
        P("nodes", "heads"),
        P("nodes", "heads"),
        P(None, "heads"),
        P(None, "heads"),
        P(None, "heads"),
        P("heads", None),
        P("nodes"),
        P("nodes", None),
    )
    return jax.shard_map(
        body,
        mesh=mesh,
        in_specs=placed,
        out_specs=(
            P("nodes", "heads"),
            P(None, "heads"),
            P(None, "heads"),
            P(None, "heads"),
            P("heads", None),
        ),
        check_vma=False,
    )
```

```python
import math

import jax
import jax.numpy as jnp
from jax import lax
from jax.experimental import pallas as pl
from jax.experimental.pallas import tpu as pltpu
from jax.sharding import PartitionSpec as P

HEAD_DIM = 64
BLOCK = 128
ROWS = 256
COLS = 128
SHARDS = 8
NZ = 8
NY = 4
NX = 4
Z_ORDER = (4, 3, 5, 2, 6, 1, 7)
Y_ORDER = (2, 1, 3)
X_ORDER = (2, 1, 3)
TOPS = (64, 96)
PIECE = 16
SCALE = HEAD_DIM ** (-0.5)
BF = jnp.bfloat16
F32 = jnp.float32
MESH = pl.DeviceIdType.MESH
NT = (((1,), (1,)), ((), ()))
TN = (((0,), (0,)), ((), ()))


def mm(a, b):
    return jnp.dot(a, b, preferred_element_type=F32)


def mm_nt(a, b):
    return lax.dot_general(a, b, NT, preferred_element_type=F32)


def mm_tn(a, b):
    return lax.dot_general(a, b, TN, preferred_element_type=F32)


def rows_of(ref):
    return math.prod(ref.shape) // COLS


class Group:
    def __init__(self, copies, index):
        self.copies, self.index, self.rows = copies, index, 0

    def send(self, src, dst, device):
        self.rows += rows_of(src)
        pltpu.make_async_remote_copy(
            src_ref=src,
            dst_ref=dst,
            send_sem=self.copies.pool(rows_of(src)),
            recv_sem=self.copies.recv.at[self.index],
            device_id=device,
            device_id_type=MESH,
        ).start()
        return self

    def wait(self):
        ref = self.copies.tally.at[0 : self.rows, :]
        pltpu.make_async_copy(ref, ref, self.copies.recv.at[self.index]).wait()


class Copies:
    def __init__(self, send, recv, tally):
        self.send, self.recv, self.tally = send, recv, tally
        self.groups, self.pools = 0, [0]

    def group(self):
        self.groups += 1
        return Group(self, self.groups - 1)

    def pool(self, rows):
        if self.pools[-1] + rows > POOL_ROWS:
            self.pools.append(0)
        self.pools[-1] += rows
        return self.send.at[len(self.pools) - 1]

    def finish(self):
        for i, rows in enumerate(self.pools):
            ref = self.tally.at[0:rows, :]
            pltpu.make_async_copy(ref, ref, self.send.at[i]).wait()


def kernel(
    x_in, g_in, wq_in, wk_in, wv_in, wo_in, live_in, win_in,
    ig_out, f_out,
    xg, gg, xo, go, xt, wq, wkv, w_t, wo, wo_t, kv, qs, bs, expo, ad, ad_other,
    dkv, dkv_other, dkv_recv, grads,
    part, ra1, rb1, ra2, rb2, fin, it_send, it_recv, it_pass, it_last, ig,
    ea1, eb1, ea2, es2, eb2, tally, live_s, win_s,
    local_sem, send_sem, recv_sem, pair_sem, out_sem,
):
    node = lax.axis_index("nodes")
    head = lax.axis_index("heads")
    core = lax.rem(node, 2)
    z = lax.rem(node // 2, NZ)
    y = node // (2 * NZ)
    nodes = 2 * NZ * NY
    xx = head // 2
    yl = lax.rem(head, 2)

    def at_z(d):
        return lax.rem(z + d, NZ)

    def at_y(d):
        return lax.rem(y + d, NY)

    def at_x(d):
        return lax.rem(xx + d, NX)

    left = (lax.rem(node + nodes - 1, nodes), head)
    right = (lax.rem(node + 1, nodes), head)
    other = (node + 1 - 2 * core, head)

    def along(steps):
        return (lax.rem(node + nodes + steps, nodes), head)


    def z_dev(d):
        return ((y * NZ + at_z(d)) * 2 + core, head)

    def y_dev(d):
        return ((at_y(d) * NZ + z) * 2 + core, head)

    def x_dev(d):
        return (node, at_x(d) * 2 + yl)

    mate_head = xx * 2 + 1 - yl
    mate = (node, mate_head)

    partners = [z_dev(d) for d in Z_ORDER] + [y_dev(d) for d in Y_ORDER]
    partners += [x_dev(d) for d in X_ORDER] + [mate, left, right, along(-2), along(2)]
    barrier = pltpu.get_barrier_semaphore()
    for dev in partners:
        pl.semaphore_signal(barrier, inc=1, device_id=dev, device_id_type=MESH)

    scalars = [
        pltpu.make_async_copy(live_in, live_s, local_sem.at[0]),
        pltpu.make_async_copy(win_in, win_s, local_sem.at[1]),
    ]
    loads = [
        pltpu.make_async_copy(x_in, xg.at[head], local_sem.at[2]),
        pltpu.make_async_copy(g_in, gg.at[head], local_sem.at[2]),
        pltpu.make_async_copy(wk_in, wkv.at[:, 0:COLS], local_sem.at[3]),
        pltpu.make_async_copy(wv_in, wkv.at[:, COLS:], local_sem.at[3]),
        pltpu.make_async_copy(wq_in, wq, local_sem.at[4]),
        pltpu.make_async_copy(wo_in, wo, local_sem.at[4]),
    ]
    for load in scalars + loads:
        load.start()

    pl.semaphore_wait(barrier, len(partners))
    copies = Copies(send_sem, recv_sem, tally)
    far = at_x(2) * 2 + yl
    x_far, x_mate, x_rest = copies.group(), copies.group(), copies.group()
    x_far.send(x_in, xg.at[head], x_dev(2))
    x_mate.send(x_in, xg.at[head], mate)
    for d in (1, 3):
        x_rest.send(x_in, xg.at[head], x_dev(d))
    g_far, g_mate, g_rest = copies.group(), copies.group(), copies.group()
    g_mate.send(g_in, gg.at[head], mate)
    for load in scalars:
        load.wait()
    live = live_s[0]
    lane_row = lax.broadcasted_iota(jnp.int32, (16, ROWS), 1)
    kv[1, ROWS : ROWS + 16, :] = jnp.where(lane_row < live, 1.0, 0.0).astype(BF)
    pltpu.make_async_copy(xg.at[0:2], xg.at[0:2], local_sem.at[2]).wait()
    pltpu.make_async_copy(wkv, wkv, local_sem.at[3]).wait()
    pltpu.make_async_copy(wkv, wkv, local_sem.at[4]).wait()

    x_mate.wait()
    for d in (1, 3):
        x_rest.send(xg.at[mate_head], xg.at[mate_head], x_dev(d))
    x_far.wait()
    x_rest.send(xg.at[far], xg.at[far], mate)
    g_far.send(g_in, gg.at[head], x_dev(2))
    for d in (1, 3):
        g_rest.send(g_in, gg.at[head], x_dev(d))
    g_mate.wait()
    for d in (1, 3):
        g_rest.send(gg.at[mate_head], gg.at[mate_head], x_dev(d))
    for s in range(SHARDS):
        rows, cols = slice(s * COLS, (s + 1) * COLS), slice((s % 2) * COLS, (s % 2 + 1) * COLS)
        w_t[s // 2, 0:COLS, cols] = wq[rows, :].T
        w_t[s // 2, COLS:, cols] = wkv[rows, :].T
    x_rest.wait()

    x_full = jnp.concatenate([xg[s] for s in range(SHARDS)], axis=1)
    kv[1, 0:ROWS, :] = mm(x_full, wkv[...]).astype(BF)
    kv_halo = copies.group()
    kv_halo.send(kv.at[1], kv.at[0], right)
    kv_halo.send(kv.at[1], kv.at[2], left)
    x_core = copies.group().send(xg, xo, other)
    g_far.wait()
    g_rest.send(gg.at[far], gg.at[far], mate)

    first = lax.broadcasted_iota(jnp.int32, (ROWS, COLS), 1) < HEAD_DIM
    queries = mm(x_full, wq[...])
    qs[0:ROWS, :] = jnp.where(first, queries, 0.0).astype(BF)
    qs[ROWS:, :] = jnp.where(first, 0.0, queries).astype(BF)

    col = lax.broadcasted_iota(jnp.int32, (ROWS, ROWS), 1)
    row = lax.broadcasted_iota(jnp.int32, (ROWS, ROWS), 0)
    col_block = lax.broadcasted_iota(jnp.int32, (1, ROWS), 1) // BLOCK

    def exponents(i):
        live_row = kv[i, ROWS : ROWS + 16, :].astype(F32)[0:1, :]
        block = col_block + 2 * (node - 1 + i)
        usable = []
        for b in range(2):
            chosen = (block == win_s[b, 0]) | (block == win_s[b, 1]) | (block == win_s[b, 2])
            usable.append(jnp.broadcast_to(jnp.where(chosen, live_row, 0.0), (BLOCK, ROWS)))
        allowed = jnp.concatenate(usable, axis=0) > 0.5
        if i == 1:
            allowed = allowed | (col == row)
        sums = []
        for h in range(2):
            rows = slice(h * ROWS, (h + 1) * ROWS)
            scores = mm_nt(qs[rows, :], kv[i, 0:ROWS, 0:COLS]) * SCALE
            value = jnp.where(allowed, jnp.exp(scores), 0.0)
            expo[i, rows, :] = value
            sums.append(jnp.sum(value, axis=-1, keepdims=True))
        return jnp.concatenate(sums, axis=0)

    total = exponents(1)
    qs_t = qs[...].T
    for s in range(SHARDS):
        wo_t[s * COLS : (s + 1) * COLS, :] = wo[:, s * COLS : (s + 1) * COLS].T
    for s in range(SHARDS):
        xt[s, :, 0:ROWS] = xg[s].T
    g_rest.wait()
    g_core = pltpu.make_async_remote_copy(
        src_ref=gg,
        dst_ref=go,
        send_sem=pair_sem.at[0],
        recv_sem=pair_sem.at[1],
        device_id=other,
        device_id_type=MESH,
    )

    @pl.when(core == 0)
    def _():
        g_core.start()

    g_full = jnp.concatenate([gg[s] for s in range(SHARDS)], axis=1)
    back = mm(g_full, wo_t[...])
    bs[0:ROWS, :] = jnp.where(first, back, 0.0).astype(BF)
    bs[ROWS:, :] = jnp.where(first, 0.0, back).astype(BF)
    bs_t = bs[...].T
    x_core.wait()
    for s in range(SHARDS):
        xt[s, :, ROWS : 2 * ROWS] = xo[s].T

    def keys(i):
        return kv[i, 0:ROWS, 0:COLS]

    def vals(i):
        return kv[i, 0:ROWS, COLS:]

    dprob = {1: mm_nt(bs[...], vals(1))}
    kv_halo.wait()
    total = total + exponents(0) + exponents(2)
    inverse = 1.0 / total
    prob, low = {}, {}
    mid_slot, off_slot = 2 - 2 * core, 2 * core
    two_slots = pl.ds(1 - core, 2)

    def to_other(src, dst, i):
        return pltpu.make_async_remote_copy(
            src_ref=src,
            dst_ref=dst,
            send_sem=pair_sem.at[i],
            recv_sem=pair_sem.at[i + 1],
            device_id=other,
            device_id_type=MESH,
        )

    dkv_copy = to_other(dkv.at[1 - core, two_slots], dkv_other, 4)
    early_copy = to_other(ad.at[1 - core], ad_other, 2)
    dkv_halo = copies.group()
    for i in (0, 2, 1):
        prob[i] = expo[i] * inverse
        low[i] = prob[i].astype(BF)
        dkv[1, i] = mm(bs_t, low[i]).astype(BF).T
        if i == 2:
            dkv_halo.send(dkv.at[1, off_slot], dkv_recv.at[core], along(3 * core - 1))

    dprob[0] = mm_nt(bs[...], vals(0))
    dprob[2] = mm_nt(bs[...], vals(2))
    delta = 0.0
    for i in range(3):
        delta = delta + jnp.sum(prob[i] * dprob[i], axis=-1, keepdims=True)
    dscore = {}
    for i in (0, 2, 1):
        dscore[i] = (SCALE * prob[i] * (dprob[i] - delta)).astype(BF)
        dkv[0, i] = mm(qs_t, dscore[i]).astype(BF).T
        if i == 2:
            dkv_halo.send(dkv.at[0, off_slot], dkv_recv.at[1 - core], along(3 * core - 2))
    dkv_copy.start()

    at = mm(low[0], vals(0)) + mm(low[1], vals(1)) + mm(low[2], vals(2))
    ad[1] = jnp.where(first, at[0:ROWS], at[ROWS:]).astype(BF)

    @pl.when(core == 0)
    def _():
        early_copy.start()

    dq = mm(dscore[0], keys(0)) + mm(dscore[1], keys(1)) + mm(dscore[2], keys(2))
    ad[0] = jnp.where(first, dq[0:ROWS], dq[ROWS:]).astype(BF)

    @pl.when(core == 1)
    def _():
        early_copy.start()


    def pair(i):
        return pl.ds(2 * i, 2)

    def to_all(devices, order, src, dst):
        group = copies.group()
        for d in order:
            group.send(src(d), dst(d), devices(d))
        return group

    def reduce_within(e, top, a_in, b_in):
        a = to_all(z_dev, Z_ORDER, lambda d: part.at[e, at_z(d), 0:top, :], lambda d: a_in.at[d])
        b = to_all(
            y_dev, Y_ORDER, lambda d: part.at[e, pair(at_y(d)), top:, :], lambda d: b_in.at[d]
        )
        return a, b

    def added(own, arrived, count):
        total = own.astype(F32)
        for d in range(1, count):
            total = total + arrived[d].astype(F32)
        return total.astype(BF)

    def added_in_order(copies_in, count):
        total = copies_in[0].astype(F32)
        for i in range(1, count):
            total = total + copies_in[i].astype(F32)
        return total.astype(BF)

    def spread(devices, order, ref):
        return to_all(devices, order, lambda d: ref, lambda d: ref)

    def hand_rows(e, group, rows, i):
        ref = f_out.at[2 * e + core]
        group.send(fin.at[e, i, rows, :], ref.at[i, rows, :], other)

    def store(e):
        out = pltpu.make_async_copy(fin.at[e], f_out.at[2 * e + core], out_sem.at[e])
        out.start()
        return out

    early_copy.wait_recv()

    @pl.when(core == 0)
    def _():
        part[0, :, :, :] = (
            mm(
                xt[...].reshape(SHARDS * COLS, 2 * ROWS),
                jnp.concatenate([ad[0], ad_other[...]], axis=0),
            )
            .astype(BF)
            .reshape(SHARDS, COLS, COLS)
        )

    @pl.when(core == 1)
    def _():
        g_core.wait_recv()
        lhs = jnp.concatenate([ad[1].T, ad_other[...].T], axis=1)
        for s in range(SHARDS):
            part[0, s] = mm(lhs, jnp.concatenate([gg[s], go[s]], axis=0)).astype(BF)

    early_a, early_b = reduce_within(0, TOPS[0], ea1, eb1)
    dkv_copy.wait_recv()
    own = dkv[core, 1].astype(F32) + dkv_other[core].astype(F32)
    across = dkv[core, mid_slot].astype(F32) + dkv_other[1 - core].astype(F32)
    dkv_halo.wait()
    grads[core] = (own + dkv_recv[0].astype(F32)).astype(BF)
    grads[2] = (across + dkv_recv[1].astype(F32)).astype(BF)
    rest_copy = copies.group().send(grads.at[2], grads.at[core], other)
    part[1, :, :, :] = (
        mm(
            xt[...].reshape(SHARDS * COLS, 2 * ROWS),
            jnp.concatenate([grads[core], grads[2]], axis=0),
        )
        .astype(BF)
        .reshape(SHARDS, COLS, COLS)
    )
    late_a, late_b = reduce_within(1, TOPS[1], ra1, rb1)
    top = TOPS[0]
    early_a.wait()
    ea2[y] = added(part[0, z, 0:top, :], ea1, NZ)
    early_a = spread(y_dev, Y_ORDER, ea2.at[y])
    early_b.wait()
    es2[...] = added(part[0, pair(y), top:, :], eb1, NY)

    def piece(i):
        return lax.rem(i, 4) * PIECE

    def es2_piece(d):
        i = at_z(d)
        return es2.at[i // 4, pl.ds(pl.multiple_of(piece(i), PIECE), PIECE), :]

    early_b = to_all(z_dev, Z_ORDER, es2_piece, lambda d: eb2.at[d])
    rest_copy.wait()
    all_grads = jnp.concatenate([ad[0], grads[0], grads[1]], axis=1)
    it_copies = copies.group()
    for d in X_ORDER:
        terms = mm(all_grads, w_t[at_x(d)]).astype(BF)
        it_send[d, 0] = terms[:, 0:COLS]
        it_send[d, 1] = terms[:, COLS:]
        it_copies.send(it_send.at[d], it_recv.at[d], x_dev(d))


    late_b.wait()
    rb2[z] = added(part[1, pair(y), TOPS[1] :, :], rb1, NY)
    late_b = spread(z_dev, Z_ORDER, rb2.at[z])
    late_a.wait()
    ra2[y] = added(part[1, z, 0 : TOPS[1], :], ra1, NZ)
    late_a = spread(y_dev, Y_ORDER, ra2.at[y])

    early_b.wait()
    own_piece = pl.ds(pl.multiple_of(piece(z), PIECE), PIECE)
    place = pl.ds(pl.multiple_of(top + piece(z), PIECE), PIECE)
    fin[0, 2 * y + z // 4, place, :] = added(es2[z // 4, own_piece, :], eb2, NZ)
    early_b = spread(z_dev, Z_ORDER, fin.at[0, 2 * y + z // 4, place, :])
    early_a.wait()
    fin[0, z, 0:top, :] = added_in_order(ea2, NY)
    early_a = spread(z_dev, Z_ORDER, fin.at[0, z, 0:top, :])

    it_own = mm(all_grads, w_t[xx])
    low_half, high_half = it_own[:, 0:COLS], it_own[:, COLS:]
    it_copies.wait()
    for d in range(1, NX):
        low_half = low_half + it_recv[d, 0].astype(F32)
        high_half = high_half + it_recv[d, 1].astype(F32)
    is_low = jnp.full((ROWS, COLS), yl, jnp.int32) == 0
    it_pass[...] = jnp.where(is_low, high_half, low_half).astype(BF)
    it_copy = copies.group().send(it_pass, it_last, mate)

    late_a.wait()
    fin[1, z, 0 : TOPS[1], :] = added_in_order(ra2, NY)
    late_far = spread(z_dev, Z_ORDER[:3], fin.at[1, z, 0 : TOPS[1], :])
    late_near = spread(z_dev, Z_ORDER[3:], fin.at[1, z, 0 : TOPS[1], :])
    early_b.wait()
    early_b = spread(y_dev, Y_ORDER, fin.at[0, pair(y), top:, :])
    late_b.wait()
    fin[1, pair(y), TOPS[1] :, :] = added_in_order(rb2, NZ)
    late_b = spread(y_dev, Y_ORDER, fin.at[1, pair(y), TOPS[1] :, :])
    it_copy.wait()
    ig[...] = (jnp.where(is_low, low_half, high_half) + it_last[...].astype(F32)).astype(BF)
    ig_copy = pltpu.make_async_copy(ig, ig_out, out_sem.at[2])
    ig_copy.start()

    handed = copies.group()
    tops, rests = pl.ds(0, TOPS[1]), pl.ds(TOPS[1], BLOCK - TOPS[1])
    hand_rows(1, handed, tops, z)
    late_near.wait()
    for d in Z_ORDER[3:]:
        hand_rows(1, handed, tops, at_z(d))
    late_b.wait()
    hand_rows(1, handed, rests, pl.ds(0, SHARDS))
    early_b.wait()
    early_a.wait()
    handed.send(fin.at[0], f_out.at[core], other)
    early_out = store(0)
    late_far.wait()
    for d in Z_ORDER[:3]:
        hand_rows(1, handed, tops, at_z(d))
    late_out = store(1)
    handed.wait()
    copies.finish()
    early_copy.wait_send()
    dkv_copy.wait_send()

    @pl.when(core == 0)
    def _():
        g_core.wait_send()

    for out in (ig_copy, early_out, late_out):
        out.wait()


POOL_ROWS = 2560
N_GROUPS = 27
N_POOLS = 7


def hand_out(ig_in, f_in, ig_out, q_out, k_out, v_out, o_out, ig, fin, sem):
    loads = [pltpu.make_async_copy(f_in.at[i], fin.at[i], sem.at[i]) for i in range(4)]
    loads.append(pltpu.make_async_copy(ig_in, ig, sem.at[4]))
    for load in loads:
        load.start()
    stores = [[(fin.at[0], q_out)]]
    stores.append([(fin.at[1, s], o_out.at[:, s * COLS : (s + 1) * COLS]) for s in range(SHARDS)])
    stores += [[(fin.at[2], k_out)], [(fin.at[3], v_out)], [(ig, ig_out)]]
    started = []
    for load, pairs in zip(loads, stores):
        load.wait()
        for src, dst in pairs:
            started.append(pltpu.make_async_copy(src, dst, sem.at[5 + len(started)]))
            started[-1].start()
    for store in started:
        store.wait()


def body(inputs, out_grad, w_query, w_key, w_value, w_out, live_rows, window_blocks):
    anyspec = pl.BlockSpec(memory_space=pl.ANY)
    vm = pltpu.VMEM
    params = pltpu.CompilerParams(
        collective_id=0, has_side_effects=True, vmem_limit_bytes=62 * 1024 * 1024
    )
    input_grad, fin = pl.pallas_call(
        kernel,
        out_shape=(
            jax.ShapeDtypeStruct((ROWS, COLS), BF),
            jax.ShapeDtypeStruct((4, SHARDS, BLOCK, COLS), BF),
        ),
        in_specs=[anyspec] * 8,
        out_specs=(anyspec, anyspec),
        scratch_shapes=[
            vm((SHARDS, ROWS, COLS), BF),
            vm((SHARDS, ROWS, COLS), BF),
            vm((SHARDS, ROWS, COLS), BF),
            vm((SHARDS, ROWS, COLS), BF),
            vm((SHARDS, COLS, 2 * ROWS), BF),
            vm((SHARDS * COLS, COLS), BF),
            vm((SHARDS * COLS, 2 * COLS), BF),
            vm((NX, 3 * COLS, 2 * COLS), BF),
            vm((COLS, SHARDS * COLS), BF),
            vm((SHARDS * COLS, COLS), BF),
            vm((3, ROWS + 16, 2 * COLS), BF),
            vm((2 * ROWS, COLS), BF),
            vm((2 * ROWS, COLS), BF),
            vm((3, 2 * ROWS, ROWS), F32),
            vm((2, ROWS, COLS), BF),
            vm((ROWS, COLS), BF),
            vm((2, 3, ROWS, COLS), BF),
            vm((2, ROWS, COLS), BF),
            vm((2, ROWS, COLS), BF),
            vm((3, ROWS, COLS), BF),
            vm((2, SHARDS, BLOCK, COLS), BF),
            vm((NZ, TOPS[1], COLS), BF),
            vm((NY, 2, BLOCK - TOPS[1], COLS), BF),
            vm((NY, TOPS[1], COLS), BF),
            vm((NZ, 2, BLOCK - TOPS[1], COLS), BF),
            vm((2, SHARDS, BLOCK, COLS), BF),
            vm((NX, 2, ROWS, COLS), BF),
            vm((NX, 2, ROWS, COLS), BF),
            vm((ROWS, COLS), BF),
            vm((ROWS, COLS), BF),
            vm((ROWS, COLS), BF),
            vm((NZ, TOPS[0], COLS), BF),
            vm((NY, 2, BLOCK - TOPS[0], COLS), BF),
            vm((NY, TOPS[0], COLS), BF),
            vm((2, BLOCK - TOPS[0], COLS), BF),
            vm((NZ, PIECE, COLS), BF),
            vm((POOL_ROWS, COLS), BF),
            pltpu.SMEM((1,), jnp.int32),
            pltpu.SMEM((2, 3), jnp.int32),
            pltpu.SemaphoreType.DMA((5,)),
            pltpu.SemaphoreType.DMA((N_POOLS,)),
            pltpu.SemaphoreType.DMA((N_GROUPS,)),
            pltpu.SemaphoreType.DMA((6,)),
            pltpu.SemaphoreType.DMA((3,)),
        ],
        compiler_params=params,
        cost_estimate=pl.CostEstimate(
            flops=1200000000, bytes_accessed=3000000, transcendentals=400000
        ),
    )(inputs, out_grad, w_query, w_key, w_value, w_out, live_rows, window_blocks)
    width = SHARDS * COLS
    cols = jax.ShapeDtypeStruct((SHARDS, COLS, COLS), BF)
    input_grad, grad_query, grad_key, grad_value, grad_out = pl.pallas_call(
        hand_out,
        out_shape=(
            jax.ShapeDtypeStruct((ROWS, COLS), BF),
            cols,
            cols,
            cols,
            jax.ShapeDtypeStruct((COLS, width), BF),
        ),
        in_specs=[anyspec] * 2,
        out_specs=[anyspec] * 5,
        scratch_shapes=[
            vm((ROWS, COLS), BF),
            vm((4, SHARDS, BLOCK, COLS), BF),
            pltpu.SemaphoreType.DMA((9 + SHARDS,)),
        ],
        compiler_params=pltpu.CompilerParams(vmem_limit_bytes=62 * 1024 * 1024),
        cost_estimate=pl.CostEstimate(flops=0, bytes_accessed=2200000, transcendentals=0),
    )(input_grad, fin)
    return (
        input_grad,
        grad_query.reshape(width, COLS),
        grad_key.reshape(width, COLS),
        grad_value.reshape(width, COLS),
        grad_out,
    )


def solution(mesh):
    placed = (
        P("nodes", "heads"),
        P("nodes", "heads"),
        P(None, "heads"),
        P(None, "heads"),
        P(None, "heads"),
        P("heads", None),
        P("nodes"),
        P("nodes", None),
    )
    return jax.shard_map(
        body,
        mesh=mesh,
        in_specs=placed,
        out_specs=(
            P("nodes", "heads"),
            P(None, "heads"),
            P(None, "heads"),
            P(None, "heads"),
            P("heads", None),
        ),
        check_vma=False,
    )
```

```python
import math

import jax
import jax.numpy as jnp
from jax import lax
from jax.experimental import pallas as pl
from jax.experimental.pallas import tpu as pltpu
from jax.sharding import PartitionSpec as P

HEAD_DIM = 64
BLOCK = 128
ROWS = 256
COLS = 128
SHARDS = 8
NZ = 8
NY = 4
NX = 4
Z_ORDER = (4, 3, 5, 2, 6, 1, 7)
Y_ORDER = (2, 1, 3)
X_ORDER = (2, 1, 3)
TOPS = (64, 96)
PIECE = 16
LATE_PART = TOPS[1] // 2
SCALE = HEAD_DIM ** (-0.5)
BF = jnp.bfloat16
F32 = jnp.float32
MESH = pl.DeviceIdType.MESH
NT = (((1,), (1,)), ((), ()))
TN = (((0,), (0,)), ((), ()))


def mm(a, b):
    return jnp.dot(a, b, preferred_element_type=F32)


def mm_nt(a, b):
    return lax.dot_general(a, b, NT, preferred_element_type=F32)


def mm_tn(a, b):
    return lax.dot_general(a, b, TN, preferred_element_type=F32)


def rows_of(ref):
    return math.prod(ref.shape) // COLS


class Group:
    def __init__(self, copies, index):
        self.copies, self.index, self.rows = copies, index, 0

    def send(self, src, dst, device):
        self.rows += rows_of(src)
        pltpu.make_async_remote_copy(
            src_ref=src,
            dst_ref=dst,
            send_sem=self.copies.pool(rows_of(src)),
            recv_sem=self.copies.recv.at[self.index],
            device_id=device,
            device_id_type=MESH,
        ).start()
        return self

    def wait(self):
        ref = self.copies.tally.at[0 : self.rows, :]
        pltpu.make_async_copy(ref, ref, self.copies.recv.at[self.index]).wait()


class Copies:
    def __init__(self, send, recv, tally):
        self.send, self.recv, self.tally = send, recv, tally
        self.groups, self.pools = 0, [0]

    def group(self):
        self.groups += 1
        return Group(self, self.groups - 1)

    def pool(self, rows):
        if self.pools[-1] + rows > POOL_ROWS:
            self.pools.append(0)
        self.pools[-1] += rows
        return self.send.at[len(self.pools) - 1]

    def finish(self):
        for i, rows in enumerate(self.pools):
            ref = self.tally.at[0:rows, :]
            pltpu.make_async_copy(ref, ref, self.send.at[i]).wait()


def kernel(
    x_in, g_in, wq_in, wk_in, wv_in, wo_in, live_in, win_in,
    ig_out, f_out,
    xg, gg, xo, go, xt, wq, wkv, w_t, wo, wo_t, kv, qs, bs, expo, ad, ad_other,
    dkv, dkv_other, dkv_recv, grads,
    part, ra1, rb1, ra2, rb2, fin, it_send, it_recv, it_pass, it_last, ig,
    ea1, eb1, ea2, es2, eb2, tally, live_s, win_s,
    local_sem, send_sem, recv_sem, pair_sem, out_sem,
):
    node = lax.axis_index("nodes")
    head = lax.axis_index("heads")
    core = lax.rem(node, 2)
    z = lax.rem(node // 2, NZ)
    y = node // (2 * NZ)
    nodes = 2 * NZ * NY
    xx = head // 2
    yl = lax.rem(head, 2)

    def at_z(d):
        return lax.rem(z + d, NZ)

    def at_y(d):
        return lax.rem(y + d, NY)

    def at_x(d):
        return lax.rem(xx + d, NX)

    left = (lax.rem(node + nodes - 1, nodes), head)
    right = (lax.rem(node + 1, nodes), head)
    other = (node + 1 - 2 * core, head)

    def along(steps):
        return (lax.rem(node + nodes + steps, nodes), head)


    def z_dev(d):
        return ((y * NZ + at_z(d)) * 2 + core, head)

    def y_dev(d):
        return ((at_y(d) * NZ + z) * 2 + core, head)

    def x_dev(d):
        return (node, at_x(d) * 2 + yl)

    mate_head = xx * 2 + 1 - yl
    mate = (node, mate_head)

    partners = [z_dev(d) for d in Z_ORDER] + [y_dev(d) for d in Y_ORDER]
    partners += [x_dev(d) for d in X_ORDER] + [mate, left, right, along(-2), along(2)]
    barrier = pltpu.get_barrier_semaphore()
    for dev in partners:
        pl.semaphore_signal(barrier, inc=1, device_id=dev, device_id_type=MESH)

    scalars = [
        pltpu.make_async_copy(live_in, live_s, local_sem.at[0]),
        pltpu.make_async_copy(win_in, win_s, local_sem.at[1]),
    ]
    loads = [
        pltpu.make_async_copy(x_in, xg.at[head], local_sem.at[2]),
        pltpu.make_async_copy(g_in, gg.at[head], local_sem.at[2]),
        pltpu.make_async_copy(wk_in, wkv.at[:, 0:COLS], local_sem.at[3]),
        pltpu.make_async_copy(wv_in, wkv.at[:, COLS:], local_sem.at[3]),
        pltpu.make_async_copy(wq_in, wq, local_sem.at[4]),
        pltpu.make_async_copy(wo_in, wo, local_sem.at[4]),
    ]
    for load in scalars + loads:
        load.start()

    pl.semaphore_wait(barrier, len(partners))
    copies = Copies(send_sem, recv_sem, tally)
    far = at_x(2) * 2 + yl
    x_far, x_mate, x_rest = copies.group(), copies.group(), copies.group()
    x_far.send(x_in, xg.at[head], x_dev(2))
    x_mate.send(x_in, xg.at[head], mate)
    for d in (1, 3):
        x_rest.send(x_in, xg.at[head], x_dev(d))
    g_far, g_mate, g_rest = copies.group(), copies.group(), copies.group()
    g_mate.send(g_in, gg.at[head], mate)
    for load in scalars:
        load.wait()
    live = live_s[0]
    lane_row = lax.broadcasted_iota(jnp.int32, (16, ROWS), 1)
    kv[1, ROWS : ROWS + 16, :] = jnp.where(lane_row < live, 1.0, 0.0).astype(BF)
    pltpu.make_async_copy(xg.at[0:2], xg.at[0:2], local_sem.at[2]).wait()
    pltpu.make_async_copy(wkv, wkv, local_sem.at[3]).wait()
    pltpu.make_async_copy(wkv, wkv, local_sem.at[4]).wait()

    x_mate.wait()
    for d in (1, 3):
        x_rest.send(xg.at[mate_head], xg.at[mate_head], x_dev(d))
    x_far.wait()
    x_rest.send(xg.at[far], xg.at[far], mate)
    g_far.send(g_in, gg.at[head], x_dev(2))
    for d in (1, 3):
        g_rest.send(g_in, gg.at[head], x_dev(d))
    g_mate.wait()
    for d in (1, 3):
        g_rest.send(gg.at[mate_head], gg.at[mate_head], x_dev(d))
    for s in range(SHARDS):
        rows, cols = slice(s * COLS, (s + 1) * COLS), slice((s % 2) * COLS, (s % 2 + 1) * COLS)
        w_t[s // 2, 0:COLS, cols] = wq[rows, :].T
        w_t[s // 2, COLS:, cols] = wkv[rows, :].T
    x_rest.wait()

    x_full = jnp.concatenate([xg[s] for s in range(SHARDS)], axis=1)
    kv[1, 0:ROWS, :] = mm(x_full, wkv[...]).astype(BF)
    kv_halo = copies.group()
    kv_halo.send(kv.at[1], kv.at[0], right)
    kv_halo.send(kv.at[1], kv.at[2], left)
    x_core = copies.group().send(xg, xo, other)
    g_far.wait()
    g_rest.send(gg.at[far], gg.at[far], mate)

    first = lax.broadcasted_iota(jnp.int32, (ROWS, COLS), 1) < HEAD_DIM
    queries = mm(x_full, wq[...])
    qs[0:ROWS, :] = jnp.where(first, queries, 0.0).astype(BF)
    qs[ROWS:, :] = jnp.where(first, 0.0, queries).astype(BF)

    col = lax.broadcasted_iota(jnp.int32, (ROWS, ROWS), 1)
    row = lax.broadcasted_iota(jnp.int32, (ROWS, ROWS), 0)
    col_block = lax.broadcasted_iota(jnp.int32, (1, ROWS), 1) // BLOCK

    def exponents(i):
        live_row = kv[i, ROWS : ROWS + 16, :].astype(F32)[0:1, :]
        block = col_block + 2 * (node - 1 + i)
        usable = []
        for b in range(2):
            chosen = (block == win_s[b, 0]) | (block == win_s[b, 1]) | (block == win_s[b, 2])
            usable.append(jnp.broadcast_to(jnp.where(chosen, live_row, 0.0), (BLOCK, ROWS)))
        allowed = jnp.concatenate(usable, axis=0) > 0.5
        if i == 1:
            allowed = allowed | (col == row)
        sums = []
        for h in range(2):
            rows = slice(h * ROWS, (h + 1) * ROWS)
            scores = mm_nt(qs[rows, :], kv[i, 0:ROWS, 0:COLS]) * SCALE
            value = jnp.where(allowed, jnp.exp(scores), 0.0)
            expo[i, rows, :] = value
            sums.append(jnp.sum(value, axis=-1, keepdims=True))
        return jnp.concatenate(sums, axis=0)

    total = exponents(1)
    qs_t = qs[...].T
    for s in range(SHARDS):
        wo_t[s * COLS : (s + 1) * COLS, :] = wo[:, s * COLS : (s + 1) * COLS].T
    for s in range(SHARDS):
        xt[s, :, 0:ROWS] = xg[s].T
    g_rest.wait()
    g_core = pltpu.make_async_remote_copy(
        src_ref=gg,
        dst_ref=go,
        send_sem=pair_sem.at[0],
        recv_sem=pair_sem.at[1],
        device_id=other,
        device_id_type=MESH,
    )

    @pl.when(core == 0)
    def _():
        g_core.start()

    g_full = jnp.concatenate([gg[s] for s in range(SHARDS)], axis=1)
    back = mm(g_full, wo_t[...])
    bs[0:ROWS, :] = jnp.where(first, back, 0.0).astype(BF)
    bs[ROWS:, :] = jnp.where(first, 0.0, back).astype(BF)
    bs_t = bs[...].T
    x_core.wait()
    for s in range(SHARDS):
        xt[s, :, ROWS : 2 * ROWS] = xo[s].T

    def keys(i):
        return kv[i, 0:ROWS, 0:COLS]

    def vals(i):
        return kv[i, 0:ROWS, COLS:]

    dprob = {1: mm_nt(bs[...], vals(1))}
    kv_halo.wait()
    total = total + exponents(0) + exponents(2)
    inverse = 1.0 / total
    prob, low = {}, {}
    mid_slot, off_slot = 2 - 2 * core, 2 * core
    two_slots = pl.ds(1 - core, 2)

    def to_other(src, dst, i):
        return pltpu.make_async_remote_copy(
            src_ref=src,
            dst_ref=dst,
            send_sem=pair_sem.at[i],
            recv_sem=pair_sem.at[i + 1],
            device_id=other,
            device_id_type=MESH,
        )

    dkv_copy = to_other(dkv.at[1 - core, two_slots], dkv_other, 4)
    early_copy = to_other(ad.at[1 - core], ad_other, 2)
    dkv_halo = copies.group()
    for i in (0, 2, 1):
        prob[i] = expo[i] * inverse
        low[i] = prob[i].astype(BF)
        dkv[1, i] = mm(bs_t, low[i]).astype(BF).T
        if i == 2:
            dkv_halo.send(dkv.at[1, off_slot], dkv_recv.at[core], along(3 * core - 1))

    dprob[0] = mm_nt(bs[...], vals(0))
    dprob[2] = mm_nt(bs[...], vals(2))
    delta = 0.0
    for i in range(3):
        delta = delta + jnp.sum(prob[i] * dprob[i], axis=-1, keepdims=True)
    dscore = {}
    for i in (0, 2, 1):
        dscore[i] = (SCALE * prob[i] * (dprob[i] - delta)).astype(BF)
        dkv[0, i] = mm(qs_t, dscore[i]).astype(BF).T
        if i == 2:
            dkv_halo.send(dkv.at[0, off_slot], dkv_recv.at[1 - core], along(3 * core - 2))
    dkv_copy.start()

    at = mm(low[0], vals(0)) + mm(low[1], vals(1)) + mm(low[2], vals(2))
    ad[1] = jnp.where(first, at[0:ROWS], at[ROWS:]).astype(BF)

    @pl.when(core == 0)
    def _():
        early_copy.start()

    dq = mm(dscore[0], keys(0)) + mm(dscore[1], keys(1)) + mm(dscore[2], keys(2))
    ad[0] = jnp.where(first, dq[0:ROWS], dq[ROWS:]).astype(BF)

    @pl.when(core == 1)
    def _():
        early_copy.start()


    def pair(i):
        return pl.ds(2 * i, 2)

    def to_all(devices, order, src, dst):
        group = copies.group()
        for d in order:
            group.send(src(d), dst(d), devices(d))
        return group

    def reduce_within(e, top, a_in, b_in):
        a = to_all(z_dev, Z_ORDER, lambda d: part.at[e, at_z(d), 0:top, :], lambda d: a_in.at[d])
        b = to_all(
            y_dev, Y_ORDER, lambda d: part.at[e, pair(at_y(d)), top:, :], lambda d: b_in.at[d]
        )
        return a, b

    def added(own, arrived, count):
        total = own.astype(F32)
        for d in range(1, count):
            total = total + arrived[d].astype(F32)
        return total.astype(BF)

    def added_in_order(copies_in, count):
        total = copies_in[0].astype(F32)
        for i in range(1, count):
            total = total + copies_in[i].astype(F32)
        return total.astype(BF)

    def spread(devices, order, ref):
        return to_all(devices, order, lambda d: ref, lambda d: ref)

    def store(e):
        out = pltpu.make_async_copy(fin.at[e], f_out.at[2 * e + core], out_sem.at[e])
        out.start()
        return out

    early_copy.wait_recv()

    @pl.when(core == 0)
    def _():
        part[0, :, :, :] = (
            mm(
                xt[...].reshape(SHARDS * COLS, 2 * ROWS),
                jnp.concatenate([ad[0], ad_other[...]], axis=0),
            )
            .astype(BF)
            .reshape(SHARDS, COLS, COLS)
        )

    @pl.when(core == 1)
    def _():
        g_core.wait_recv()
        lhs = jnp.concatenate([ad[1].T, ad_other[...].T], axis=1)
        for s in range(SHARDS):
            part[0, s] = mm(lhs, jnp.concatenate([gg[s], go[s]], axis=0)).astype(BF)

    early_a, early_b = reduce_within(0, TOPS[0], ea1, eb1)
    dkv_copy.wait_recv()
    own = dkv[core, 1].astype(F32) + dkv_other[core].astype(F32)
    across = dkv[core, mid_slot].astype(F32) + dkv_other[1 - core].astype(F32)
    dkv_halo.wait()
    grads[core] = (own + dkv_recv[0].astype(F32)).astype(BF)
    grads[2] = (across + dkv_recv[1].astype(F32)).astype(BF)
    rest_copy = copies.group().send(grads.at[2], grads.at[core], other)
    part[1, :, :, :] = (
        mm(
            xt[...].reshape(SHARDS * COLS, 2 * ROWS),
            jnp.concatenate([grads[core], grads[2]], axis=0),
        )
        .astype(BF)
        .reshape(SHARDS, COLS, COLS)
    )
    def late_part(i):
        return slice(i * LATE_PART, (i + 1) * LATE_PART)

    def late_reduce(i):
        return to_all(
            z_dev, Z_ORDER, lambda d: part.at[1, at_z(d), late_part(i), :], lambda d: ra1.at[i, d]
        )

    late_0 = late_reduce(0)
    late_b = to_all(
        y_dev, Y_ORDER, lambda d: part.at[1, pair(at_y(d)), TOPS[1] :, :], lambda d: rb1.at[d]
    )
    late_1 = late_reduce(1)
    top = TOPS[0]
    early_a.wait()
    ea2[y] = added(part[0, z, 0:top, :], ea1, NZ)
    early_a = spread(y_dev, Y_ORDER, ea2.at[y])
    early_b.wait()
    es2[...] = added(part[0, pair(y), top:, :], eb1, NY)

    def piece(i):
        return lax.rem(i, 4) * PIECE

    def es2_piece(d):
        i = at_z(d)
        return es2.at[i // 4, pl.ds(pl.multiple_of(piece(i), PIECE), PIECE), :]

    early_b = to_all(z_dev, Z_ORDER, es2_piece, lambda d: eb2.at[d])
    rest_copy.wait()
    all_grads = jnp.concatenate([ad[0], grads[0], grads[1]], axis=1)
    it_copies = copies.group()
    for d in X_ORDER:
        terms = mm(all_grads, w_t[at_x(d)]).astype(BF)
        it_send[d, 0] = terms[:, 0:COLS]
        it_send[d, 1] = terms[:, COLS:]
        it_copies.send(it_send.at[d], it_recv.at[d], x_dev(d))


    late_b.wait()
    rb2[z] = added(part[1, pair(y), TOPS[1] :, :], rb1, NY)
    late_b = spread(z_dev, Z_ORDER, rb2.at[z])
    def late_exchange(i):
        ra2[i, y] = added(part[1, z, late_part(i), :], ra1.at[i], NZ)
        return spread(y_dev, Y_ORDER, ra2.at[i, y])

    def late_gather(i):
        fin[1, z, late_part(i), :] = added_in_order(ra2.at[i], NY)
        return spread(z_dev, Z_ORDER, fin.at[1, z, late_part(i), :])

    late_0.wait()
    late_0 = late_exchange(0)

    early_b.wait()
    own_piece = pl.ds(pl.multiple_of(piece(z), PIECE), PIECE)
    place = pl.ds(pl.multiple_of(top + piece(z), PIECE), PIECE)
    fin[0, 2 * y + z // 4, place, :] = added(es2[z // 4, own_piece, :], eb2, NZ)
    early_b = spread(z_dev, Z_ORDER, fin.at[0, 2 * y + z // 4, place, :])
    early_a.wait()
    fin[0, z, 0:top, :] = added_in_order(ea2, NY)
    early_a = spread(z_dev, Z_ORDER, fin.at[0, z, 0:top, :])
    late_1.wait()
    late_1 = late_exchange(1)

    late_0.wait()
    late_0 = late_gather(0)
    early_b.wait()
    early_b = spread(y_dev, Y_ORDER, fin.at[0, pair(y), top:, :])
    late_b.wait()
    fin[1, pair(y), TOPS[1] :, :] = added_in_order(rb2, NZ)
    late_b = spread(y_dev, Y_ORDER, fin.at[1, pair(y), TOPS[1] :, :])
    late_1.wait()
    late_1 = late_gather(1)

    it_own = mm(all_grads, w_t[xx])
    low_half, high_half = it_own[:, 0:COLS], it_own[:, COLS:]
    it_copies.wait()
    for d in range(1, NX):
        low_half = low_half + it_recv[d, 0].astype(F32)
        high_half = high_half + it_recv[d, 1].astype(F32)
    is_low = jnp.full((ROWS, COLS), yl, jnp.int32) == 0
    it_pass[...] = jnp.where(is_low, high_half, low_half).astype(BF)
    it_copy = copies.group().send(it_pass, it_last, mate)

    it_copy.wait()
    ig[...] = (jnp.where(is_low, low_half, high_half) + it_last[...].astype(F32)).astype(BF)
    ig_copy = pltpu.make_async_copy(ig, ig_out, out_sem.at[2])
    ig_copy.start()

    handed = copies.group()

    def hand(e, rows):
        handed.send(fin.at[e, :, rows, :], f_out.at[2 * e + core, :, rows, :], other)

    early_a.wait()
    hand(0, slice(0, top))
    late_b.wait()
    hand(1, slice(TOPS[1], BLOCK))
    late_0.wait()
    hand(1, late_part(0))
    early_b.wait()
    hand(0, slice(top, BLOCK))
    early_out = store(0)
    late_1.wait()
    hand(1, late_part(1))
    late_out = store(1)
    handed.wait()
    copies.finish()
    early_copy.wait_send()
    dkv_copy.wait_send()

    @pl.when(core == 0)
    def _():
        g_core.wait_send()

    for out in (ig_copy, early_out, late_out):
        out.wait()


POOL_ROWS = 2560
N_GROUPS = 29
N_POOLS = 7


def hand_out(ig_in, f_in, ig_out, q_out, k_out, v_out, o_out, ig, fin, sem):
    loads = [pltpu.make_async_copy(f_in.at[i], fin.at[i], sem.at[i]) for i in range(4)]
    loads.append(pltpu.make_async_copy(ig_in, ig, sem.at[4]))
    for load in loads:
        load.start()
    stores = [[(fin.at[0], q_out)]]
    stores.append([(fin.at[1, s], o_out.at[:, s * COLS : (s + 1) * COLS]) for s in range(SHARDS)])
    stores += [[(fin.at[2], k_out)], [(fin.at[3], v_out)], [(ig, ig_out)]]
    started = []
    for load, pairs in zip(loads, stores):
        load.wait()
        for src, dst in pairs:
            started.append(pltpu.make_async_copy(src, dst, sem.at[5 + len(started)]))
            started[-1].start()
    for store in started:
        store.wait()


def body(inputs, out_grad, w_query, w_key, w_value, w_out, live_rows, window_blocks):
    anyspec = pl.BlockSpec(memory_space=pl.ANY)
    vm = pltpu.VMEM
    params = pltpu.CompilerParams(
        collective_id=0, has_side_effects=True, vmem_limit_bytes=62 * 1024 * 1024
    )
    input_grad, fin = pl.pallas_call(
        kernel,
        out_shape=(
            jax.ShapeDtypeStruct((ROWS, COLS), BF),
            jax.ShapeDtypeStruct((4, SHARDS, BLOCK, COLS), BF),
        ),
        in_specs=[anyspec] * 8,
        out_specs=(anyspec, anyspec),
        scratch_shapes=[
            vm((SHARDS, ROWS, COLS), BF),
            vm((SHARDS, ROWS, COLS), BF),
            vm((SHARDS, ROWS, COLS), BF),
            vm((SHARDS, ROWS, COLS), BF),
            vm((SHARDS, COLS, 2 * ROWS), BF),
            vm((SHARDS * COLS, COLS), BF),
            vm((SHARDS * COLS, 2 * COLS), BF),
            vm((NX, 3 * COLS, 2 * COLS), BF),
            vm((COLS, SHARDS * COLS), BF),
            vm((SHARDS * COLS, COLS), BF),
            vm((3, ROWS + 16, 2 * COLS), BF),
            vm((2 * ROWS, COLS), BF),
            vm((2 * ROWS, COLS), BF),
            vm((3, 2 * ROWS, ROWS), F32),
            vm((2, ROWS, COLS), BF),
            vm((ROWS, COLS), BF),
            vm((2, 3, ROWS, COLS), BF),
            vm((2, ROWS, COLS), BF),
            vm((2, ROWS, COLS), BF),
            vm((3, ROWS, COLS), BF),
            vm((2, SHARDS, BLOCK, COLS), BF),
            vm((2, NZ, LATE_PART, COLS), BF),
            vm((NY, 2, BLOCK - TOPS[1], COLS), BF),
            vm((2, NY, LATE_PART, COLS), BF),
            vm((NZ, 2, BLOCK - TOPS[1], COLS), BF),
            vm((2, SHARDS, BLOCK, COLS), BF),
            vm((NX, 2, ROWS, COLS), BF),
            vm((NX, 2, ROWS, COLS), BF),
            vm((ROWS, COLS), BF),
            vm((ROWS, COLS), BF),
            vm((ROWS, COLS), BF),
            vm((NZ, TOPS[0], COLS), BF),
            vm((NY, 2, BLOCK - TOPS[0], COLS), BF),
            vm((NY, TOPS[0], COLS), BF),
            vm((2, BLOCK - TOPS[0], COLS), BF),
            vm((NZ, PIECE, COLS), BF),
            vm((POOL_ROWS, COLS), BF),
            pltpu.SMEM((1,), jnp.int32),
            pltpu.SMEM((2, 3), jnp.int32),
            pltpu.SemaphoreType.DMA((5,)),
            pltpu.SemaphoreType.DMA((N_POOLS,)),
            pltpu.SemaphoreType.DMA((N_GROUPS,)),
            pltpu.SemaphoreType.DMA((6,)),
            pltpu.SemaphoreType.DMA((3,)),
        ],
        compiler_params=params,
        cost_estimate=pl.CostEstimate(
            flops=1200000000, bytes_accessed=3000000, transcendentals=400000
        ),
    )(inputs, out_grad, w_query, w_key, w_value, w_out, live_rows, window_blocks)
    width = SHARDS * COLS
    cols = jax.ShapeDtypeStruct((SHARDS, COLS, COLS), BF)
    input_grad, grad_query, grad_key, grad_value, grad_out = pl.pallas_call(
        hand_out,
        out_shape=(
            jax.ShapeDtypeStruct((ROWS, COLS), BF),
            cols,
            cols,
            cols,
            jax.ShapeDtypeStruct((COLS, width), BF),
        ),
        in_specs=[anyspec] * 2,
        out_specs=[anyspec] * 5,
        scratch_shapes=[
            vm((ROWS, COLS), BF),
            vm((4, SHARDS, BLOCK, COLS), BF),
            pltpu.SemaphoreType.DMA((9 + SHARDS,)),
        ],
        compiler_params=pltpu.CompilerParams(vmem_limit_bytes=62 * 1024 * 1024),
        cost_estimate=pl.CostEstimate(flops=0, bytes_accessed=2200000, transcendentals=0),
    )(input_grad, fin)
    return (
        input_grad,
        grad_query.reshape(width, COLS),
        grad_key.reshape(width, COLS),
        grad_value.reshape(width, COLS),
        grad_out,
    )


def solution(mesh):
    placed = (
        P("nodes", "heads"),
        P("nodes", "heads"),
        P(None, "heads"),
        P(None, "heads"),
        P(None, "heads"),
        P("heads", None),
        P("nodes"),
        P("nodes", None),
    )
    return jax.shard_map(
        body,
        mesh=mesh,
        in_specs=placed,
        out_specs=(
            P("nodes", "heads"),
            P(None, "heads"),
            P(None, "heads"),
            P(None, "heads"),
            P("heads", None),
        ),
        check_vma=False,
    )
```

```python
import math

import jax
import jax.numpy as jnp
from jax import lax
from jax.experimental import pallas as pl
from jax.experimental.pallas import tpu as pltpu
from jax.sharding import PartitionSpec as P

HEAD_DIM = 64
BLOCK = 128
ROWS = 256
COLS = 128
SHARDS = 8
NZ = 8
NY = 4
NX = 4
Z_ORDER = (4, 3, 5, 2, 6, 1, 7)
Y_ORDER = (2, 1, 3)
X_ORDER = (2, 1, 3)
TOPS = (64, 96)
PIECE = 16
LATE_PART = TOPS[1] // 2
SCALE = HEAD_DIM ** (-0.5)
BF = jnp.bfloat16
F32 = jnp.float32
MESH = pl.DeviceIdType.MESH
NT = (((1,), (1,)), ((), ()))
TN = (((0,), (0,)), ((), ()))


def mm(a, b):
    return jnp.dot(a, b, preferred_element_type=F32)


def mm_nt(a, b):
    return lax.dot_general(a, b, NT, preferred_element_type=F32)


def mm_tn(a, b):
    return lax.dot_general(a, b, TN, preferred_element_type=F32)


def rows_of(ref):
    return math.prod(ref.shape) // COLS


class Group:
    def __init__(self, copies, index):
        self.copies, self.index, self.rows = copies, index, 0

    def send(self, src, dst, device):
        self.rows += rows_of(src)
        pltpu.make_async_remote_copy(
            src_ref=src,
            dst_ref=dst,
            send_sem=self.copies.pool(rows_of(src)),
            recv_sem=self.copies.recv.at[self.index],
            device_id=device,
            device_id_type=MESH,
        ).start()
        return self

    def wait(self):
        ref = self.copies.tally.at[0 : self.rows, :]
        pltpu.make_async_copy(ref, ref, self.copies.recv.at[self.index]).wait()


class Copies:
    def __init__(self, send, recv, tally):
        self.send, self.recv, self.tally = send, recv, tally
        self.groups, self.pools = 0, [0]

    def group(self):
        self.groups += 1
        return Group(self, self.groups - 1)

    def pool(self, rows):
        if self.pools[-1] + rows > POOL_ROWS:
            self.pools.append(0)
        self.pools[-1] += rows
        return self.send.at[len(self.pools) - 1]

    def finish(self):
        for i, rows in enumerate(self.pools):
            ref = self.tally.at[0:rows, :]
            pltpu.make_async_copy(ref, ref, self.send.at[i]).wait()


def kernel(
    x_in, g_in, wq_in, wk_in, wv_in, wo_in, live_in, win_in,
    ig_out, f_out,
    xg, gg, xo, go, xt, wq, wkv, w_t, wo, wo_t, kv, qs, bs, expo, ad, ad_other,
    dkv, dkv_other, dkv_recv, grads,
    part, ra1, rb1, ra2, rb2, fin, it_send, it_recv, it_pass, it_last, ig,
    ea1, eb1, ea2, es2, eb2, tally, live_s, win_s,
    local_sem, send_sem, recv_sem, pair_sem, out_sem,
):
    node = lax.axis_index("nodes")
    head = lax.axis_index("heads")
    core = lax.rem(node, 2)
    z = lax.rem(node // 2, NZ)
    y = node // (2 * NZ)
    nodes = 2 * NZ * NY
    xx = head // 2
    yl = lax.rem(head, 2)

    def at_z(d):
        return lax.rem(z + d, NZ)

    def at_y(d):
        return lax.rem(y + d, NY)

    def at_x(d):
        return lax.rem(xx + d, NX)

    left = (lax.rem(node + nodes - 1, nodes), head)
    right = (lax.rem(node + 1, nodes), head)
    other = (node + 1 - 2 * core, head)

    def along(steps):
        return (lax.rem(node + nodes + steps, nodes), head)


    def z_dev(d):
        return ((y * NZ + at_z(d)) * 2 + core, head)

    def y_dev(d):
        return ((at_y(d) * NZ + z) * 2 + core, head)

    def x_dev(d):
        return (node, at_x(d) * 2 + yl)

    mate_head = xx * 2 + 1 - yl
    mate = (node, mate_head)

    partners = [z_dev(d) for d in Z_ORDER] + [y_dev(d) for d in Y_ORDER]
    partners += [x_dev(d) for d in X_ORDER] + [mate, left, right, along(-2), along(2)]
    barrier = pltpu.get_barrier_semaphore()
    for dev in partners:
        pl.semaphore_signal(barrier, inc=1, device_id=dev, device_id_type=MESH)

    scalars = [
        pltpu.make_async_copy(live_in, live_s, local_sem.at[0]),
        pltpu.make_async_copy(win_in, win_s, local_sem.at[1]),
    ]
    loads = [
        pltpu.make_async_copy(x_in, xg.at[head], local_sem.at[2]),
        pltpu.make_async_copy(g_in, gg.at[head], local_sem.at[2]),
        pltpu.make_async_copy(wk_in, wkv.at[:, 0:COLS], local_sem.at[3]),
        pltpu.make_async_copy(wv_in, wkv.at[:, COLS:], local_sem.at[3]),
        pltpu.make_async_copy(wq_in, wq, local_sem.at[4]),
        pltpu.make_async_copy(wo_in, wo, local_sem.at[4]),
    ]
    for load in scalars + loads:
        load.start()

    pl.semaphore_wait(barrier, len(partners))
    copies = Copies(send_sem, recv_sem, tally)
    far = at_x(2) * 2 + yl
    x_far, x_mate, x_rest = copies.group(), copies.group(), copies.group()
    x_far.send(x_in, xg.at[head], x_dev(2))
    x_mate.send(x_in, xg.at[head], mate)
    for d in (1, 3):
        x_rest.send(x_in, xg.at[head], x_dev(d))
    g_far, g_mate, g_rest = copies.group(), copies.group(), copies.group()
    g_mate.send(g_in, gg.at[head], mate)
    for load in scalars:
        load.wait()
    live = live_s[0]
    lane_row = lax.broadcasted_iota(jnp.int32, (16, ROWS), 1)
    kv[1, ROWS : ROWS + 16, :] = jnp.where(lane_row < live, 1.0, 0.0).astype(BF)
    pltpu.make_async_copy(xg.at[0:2], xg.at[0:2], local_sem.at[2]).wait()
    pltpu.make_async_copy(wkv, wkv, local_sem.at[3]).wait()
    pltpu.make_async_copy(wkv, wkv, local_sem.at[4]).wait()

    x_mate.wait()
    for d in (1, 3):
        x_rest.send(xg.at[mate_head], xg.at[mate_head], x_dev(d))
    x_far.wait()
    x_rest.send(xg.at[far], xg.at[far], mate)
    g_far.send(g_in, gg.at[head], x_dev(2))
    for d in (1, 3):
        g_rest.send(g_in, gg.at[head], x_dev(d))
    g_mate.wait()
    for d in (1, 3):
        g_rest.send(gg.at[mate_head], gg.at[mate_head], x_dev(d))
    x_rest.wait()

    x_full = jnp.concatenate([xg[s] for s in range(SHARDS)], axis=1)
    kv[1, 0:ROWS, :] = mm(x_full, wkv[...]).astype(BF)
    kv_halo = copies.group()
    kv_halo.send(kv.at[1], kv.at[0], right)
    kv_halo.send(kv.at[1], kv.at[2], left)
    x_core = copies.group().send(xg, xo, other)
    g_far.wait()
    g_rest.send(gg.at[far], gg.at[far], mate)

    first = lax.broadcasted_iota(jnp.int32, (ROWS, COLS), 1) < HEAD_DIM
    queries = mm(x_full, wq[...])
    qs[0:ROWS, :] = jnp.where(first, queries, 0.0).astype(BF)
    qs[ROWS:, :] = jnp.where(first, 0.0, queries).astype(BF)

    col = lax.broadcasted_iota(jnp.int32, (ROWS, ROWS), 1)
    row = lax.broadcasted_iota(jnp.int32, (ROWS, ROWS), 0)
    col_block = lax.broadcasted_iota(jnp.int32, (1, ROWS), 1) // BLOCK

    def exponents(i):
        live_row = kv[i, ROWS : ROWS + 16, :].astype(F32)[0:1, :]
        block = col_block + 2 * (node - 1 + i)
        usable = []
        for b in range(2):
            chosen = (block == win_s[b, 0]) | (block == win_s[b, 1]) | (block == win_s[b, 2])
            usable.append(jnp.broadcast_to(jnp.where(chosen, live_row, 0.0), (BLOCK, ROWS)))
        allowed = jnp.concatenate(usable, axis=0) > 0.5
        if i == 1:
            allowed = allowed | (col == row)
        sums = []
        for h in range(2):
            rows = slice(h * ROWS, (h + 1) * ROWS)
            scores = mm_nt(qs[rows, :], kv[i, 0:ROWS, 0:COLS]) * SCALE
            value = jnp.where(allowed, jnp.exp(scores), 0.0)
            expo[i, rows, :] = value
            sums.append(jnp.sum(value, axis=-1, keepdims=True))
        return jnp.concatenate(sums, axis=0)

    total = exponents(1)
    qs_t = qs[...].T
    for s in range(SHARDS):
        wo_t[s * COLS : (s + 1) * COLS, :] = wo[:, s * COLS : (s + 1) * COLS].T
    for s in range(SHARDS):
        xt[s, :, 0:ROWS] = xg[s].T
    g_rest.wait()
    g_core = pltpu.make_async_remote_copy(
        src_ref=gg,
        dst_ref=go,
        send_sem=pair_sem.at[0],
        recv_sem=pair_sem.at[1],
        device_id=other,
        device_id_type=MESH,
    )

    @pl.when(core == 0)
    def _():
        g_core.start()

    g_full = jnp.concatenate([gg[s] for s in range(SHARDS)], axis=1)
    back = mm(g_full, wo_t[...])
    bs[0:ROWS, :] = jnp.where(first, back, 0.0).astype(BF)
    bs[ROWS:, :] = jnp.where(first, 0.0, back).astype(BF)
    bs_t = bs[...].T
    x_core.wait()
    for s in range(SHARDS):
        xt[s, :, ROWS : 2 * ROWS] = xo[s].T

    def keys(i):
        return kv[i, 0:ROWS, 0:COLS]

    def vals(i):
        return kv[i, 0:ROWS, COLS:]

    dprob = {1: mm_nt(bs[...], vals(1))}
    kv_halo.wait()
    total = total + exponents(0) + exponents(2)
    inverse = 1.0 / total
    prob, low = {}, {}
    mid_slot, off_slot = 2 - 2 * core, 2 * core
    two_slots = pl.ds(1 - core, 2)

    def to_other(src, dst, i):
        return pltpu.make_async_remote_copy(
            src_ref=src,
            dst_ref=dst,
            send_sem=pair_sem.at[i],
            recv_sem=pair_sem.at[i + 1],
            device_id=other,
            device_id_type=MESH,
        )

    dkv_copy = to_other(dkv.at[1 - core, two_slots], dkv_other, 4)
    early_copy = to_other(ad.at[1 - core], ad_other, 2)
    dkv_halo = copies.group()
    for i in (0, 2, 1):
        prob[i] = expo[i] * inverse
        low[i] = prob[i].astype(BF)
        dkv[1, i] = mm(bs_t, low[i]).astype(BF).T
        if i == 2:
            dkv_halo.send(dkv.at[1, off_slot], dkv_recv.at[core], along(3 * core - 1))

    dprob[0] = mm_nt(bs[...], vals(0))
    dprob[2] = mm_nt(bs[...], vals(2))
    delta = 0.0
    for i in range(3):
        delta = delta + jnp.sum(prob[i] * dprob[i], axis=-1, keepdims=True)
    dscore = {}
    for i in (0, 2, 1):
        dscore[i] = (SCALE * prob[i] * (dprob[i] - delta)).astype(BF)
        dkv[0, i] = mm(qs_t, dscore[i]).astype(BF).T
        if i == 2:
            dkv_halo.send(dkv.at[0, off_slot], dkv_recv.at[1 - core], along(3 * core - 2))
    dkv_copy.start()

    at = mm(low[0], vals(0)) + mm(low[1], vals(1)) + mm(low[2], vals(2))
    ad[1] = jnp.where(first, at[0:ROWS], at[ROWS:]).astype(BF)

    @pl.when(core == 0)
    def _():
        early_copy.start()

    dq = mm(dscore[0], keys(0)) + mm(dscore[1], keys(1)) + mm(dscore[2], keys(2))
    ad[0] = jnp.where(first, dq[0:ROWS], dq[ROWS:]).astype(BF)

    @pl.when(core == 1)
    def _():
        early_copy.start()


    def pair(i):
        return pl.ds(2 * i, 2)

    def to_all(devices, order, src, dst):
        group = copies.group()
        for d in order:
            group.send(src(d), dst(d), devices(d))
        return group

    def reduce_within(e, top, a_in, b_in):
        a = to_all(z_dev, Z_ORDER, lambda d: part.at[e, at_z(d), 0:top, :], lambda d: a_in.at[d])
        b = to_all(
            y_dev, Y_ORDER, lambda d: part.at[e, pair(at_y(d)), top:, :], lambda d: b_in.at[d]
        )
        return a, b

    def added(own, arrived, count):
        total = own.astype(F32)
        for d in range(1, count):
            total = total + arrived[d].astype(F32)
        return total.astype(BF)

    def added_in_order(copies_in, count):
        total = copies_in[0].astype(F32)
        for i in range(1, count):
            total = total + copies_in[i].astype(F32)
        return total.astype(BF)

    def spread(devices, order, ref):
        return to_all(devices, order, lambda d: ref, lambda d: ref)

    def store(e):
        out = pltpu.make_async_copy(fin.at[e], f_out.at[2 * e + core], out_sem.at[e])
        out.start()
        return out

    early_copy.wait_recv()

    @pl.when(core == 0)
    def _():
        part[0, :, :, :] = (
            mm(
                xt[...].reshape(SHARDS * COLS, 2 * ROWS),
                jnp.concatenate([ad[0], ad_other[...]], axis=0),
            )
            .astype(BF)
            .reshape(SHARDS, COLS, COLS)
        )

    @pl.when(core == 1)
    def _():
        g_core.wait_recv()
        lhs = jnp.concatenate([ad[1].T, ad_other[...].T], axis=1)
        for s in range(SHARDS):
            part[0, s] = mm(lhs, jnp.concatenate([gg[s], go[s]], axis=0)).astype(BF)

    early_a, early_b = reduce_within(0, TOPS[0], ea1, eb1)
    dkv_copy.wait_recv()
    own = dkv[core, 1].astype(F32) + dkv_other[core].astype(F32)
    across = dkv[core, mid_slot].astype(F32) + dkv_other[1 - core].astype(F32)
    for s in range(SHARDS):
        rows, cols = slice(s * COLS, (s + 1) * COLS), slice((s % 2) * COLS, (s % 2 + 1) * COLS)
        w_t[s // 2, 0:COLS, cols] = wq[rows, :].T
        w_t[s // 2, COLS:, cols] = wkv[rows, :].T
    dkv_halo.wait()
    grads[core] = (own + dkv_recv[0].astype(F32)).astype(BF)
    grads[2] = (across + dkv_recv[1].astype(F32)).astype(BF)
    rest_copy = copies.group().send(grads.at[2], grads.at[core], other)
    part[1, :, :, :] = (
        mm(
            xt[...].reshape(SHARDS * COLS, 2 * ROWS),
            jnp.concatenate([grads[core], grads[2]], axis=0),
        )
        .astype(BF)
        .reshape(SHARDS, COLS, COLS)
    )
    def late_part(i):
        return slice(i * LATE_PART, (i + 1) * LATE_PART)

    def late_reduce(i):
        return to_all(
            z_dev, Z_ORDER, lambda d: part.at[1, at_z(d), late_part(i), :], lambda d: ra1.at[i, d]
        )

    late_0 = late_reduce(0)
    late_b = to_all(
        y_dev, Y_ORDER, lambda d: part.at[1, pair(at_y(d)), TOPS[1] :, :], lambda d: rb1.at[d]
    )
    late_1 = late_reduce(1)
    top = TOPS[0]
    early_a.wait()
    ea2[y] = added(part[0, z, 0:top, :], ea1, NZ)
    early_a = spread(y_dev, Y_ORDER, ea2.at[y])
    early_b.wait()
    es2[...] = added(part[0, pair(y), top:, :], eb1, NY)

    def piece(i):
        return lax.rem(i, 4) * PIECE

    def es2_piece(d):
        i = at_z(d)
        return es2.at[i // 4, pl.ds(pl.multiple_of(piece(i), PIECE), PIECE), :]

    early_b = to_all(z_dev, Z_ORDER, es2_piece, lambda d: eb2.at[d])
    rest_copy.wait()
    all_grads = jnp.concatenate([ad[0], grads[0], grads[1]], axis=1)
    it_copies = copies.group()
    for d in X_ORDER:
        terms = mm(all_grads, w_t[at_x(d)]).astype(BF)
        it_send[d, 0] = terms[:, 0:COLS]
        it_send[d, 1] = terms[:, COLS:]
        it_copies.send(it_send.at[d], it_recv.at[d], x_dev(d))


    late_b.wait()
    rb2[z] = added(part[1, pair(y), TOPS[1] :, :], rb1, NY)
    late_b = spread(z_dev, Z_ORDER, rb2.at[z])
    def late_exchange(i):
        ra2[i, y] = added(part[1, z, late_part(i), :], ra1.at[i], NZ)
        return spread(y_dev, Y_ORDER, ra2.at[i, y])

    def late_gather(i):
        fin[1, z, late_part(i), :] = added_in_order(ra2.at[i], NY)
        return spread(z_dev, Z_ORDER, fin.at[1, z, late_part(i), :])

    late_0.wait()
    late_0 = late_exchange(0)

    early_b.wait()
    own_piece = pl.ds(pl.multiple_of(piece(z), PIECE), PIECE)
    place = pl.ds(pl.multiple_of(top + piece(z), PIECE), PIECE)
    fin[0, 2 * y + z // 4, place, :] = added(es2[z // 4, own_piece, :], eb2, NZ)
    early_b = spread(z_dev, Z_ORDER, fin.at[0, 2 * y + z // 4, place, :])
    early_a.wait()
    fin[0, z, 0:top, :] = added_in_order(ea2, NY)
    early_a = spread(z_dev, Z_ORDER, fin.at[0, z, 0:top, :])
    late_1.wait()
    late_1 = late_exchange(1)

    late_0.wait()
    late_0 = late_gather(0)
    early_b.wait()
    early_b = spread(y_dev, Y_ORDER, fin.at[0, pair(y), top:, :])
    late_b.wait()
    fin[1, pair(y), TOPS[1] :, :] = added_in_order(rb2, NZ)
    late_b = spread(y_dev, Y_ORDER, fin.at[1, pair(y), TOPS[1] :, :])
    late_1.wait()
    late_1 = late_gather(1)

    it_own = mm(all_grads, w_t[xx])
    low_half, high_half = it_own[:, 0:COLS], it_own[:, COLS:]
    it_copies.wait()
    for d in range(1, NX):
        low_half = low_half + it_recv[d, 0].astype(F32)
        high_half = high_half + it_recv[d, 1].astype(F32)
    is_low = jnp.full((ROWS, COLS), yl, jnp.int32) == 0
    it_pass[...] = jnp.where(is_low, high_half, low_half).astype(BF)
    it_copy = copies.group().send(it_pass, it_last, mate)

    it_copy.wait()
    ig[...] = (jnp.where(is_low, low_half, high_half) + it_last[...].astype(F32)).astype(BF)
    ig_copy = pltpu.make_async_copy(ig, ig_out, out_sem.at[2])
    ig_copy.start()

    handed = copies.group()

    def hand(e, rows):
        handed.send(fin.at[e, :, rows, :], f_out.at[2 * e + core, :, rows, :], other)

    early_a.wait()
    hand(0, slice(0, top))
    late_b.wait()
    hand(1, slice(TOPS[1], BLOCK))
    late_0.wait()
    hand(1, late_part(0))
    early_b.wait()
    hand(0, slice(top, BLOCK))
    early_out = store(0)
    late_1.wait()
    hand(1, late_part(1))
    late_out = store(1)
    handed.wait()
    copies.finish()
    early_copy.wait_send()
    dkv_copy.wait_send()

    @pl.when(core == 0)
    def _():
        g_core.wait_send()

    for out in (ig_copy, early_out, late_out):
        out.wait()


POOL_ROWS = 2560
N_GROUPS = 29
N_POOLS = 7


def hand_out(ig_in, f_in, ig_out, q_out, k_out, v_out, o_out, ig, fin, sem):
    loads = [pltpu.make_async_copy(f_in.at[i], fin.at[i], sem.at[i]) for i in range(4)]
    loads.append(pltpu.make_async_copy(ig_in, ig, sem.at[4]))
    for load in loads:
        load.start()
    stores = [[(fin.at[0], q_out)]]
    stores.append([(fin.at[1, s], o_out.at[:, s * COLS : (s + 1) * COLS]) for s in range(SHARDS)])
    stores += [[(fin.at[2], k_out)], [(fin.at[3], v_out)], [(ig, ig_out)]]
    started = []
    for load, pairs in zip(loads, stores):
        load.wait()
        for src, dst in pairs:
            started.append(pltpu.make_async_copy(src, dst, sem.at[5 + len(started)]))
            started[-1].start()
    for store in started:
        store.wait()


def body(inputs, out_grad, w_query, w_key, w_value, w_out, live_rows, window_blocks):
    anyspec = pl.BlockSpec(memory_space=pl.ANY)
    vm = pltpu.VMEM
    params = pltpu.CompilerParams(
        collective_id=0, has_side_effects=True, vmem_limit_bytes=62 * 1024 * 1024
    )
    input_grad, fin = pl.pallas_call(
        kernel,
        out_shape=(
            jax.ShapeDtypeStruct((ROWS, COLS), BF),
            jax.ShapeDtypeStruct((4, SHARDS, BLOCK, COLS), BF),
        ),
        in_specs=[anyspec] * 8,
        out_specs=(anyspec, anyspec),
        scratch_shapes=[
            vm((SHARDS, ROWS, COLS), BF),
            vm((SHARDS, ROWS, COLS), BF),
            vm((SHARDS, ROWS, COLS), BF),
            vm((SHARDS, ROWS, COLS), BF),
            vm((SHARDS, COLS, 2 * ROWS), BF),
            vm((SHARDS * COLS, COLS), BF),
            vm((SHARDS * COLS, 2 * COLS), BF),
            vm((NX, 3 * COLS, 2 * COLS), BF),
            vm((COLS, SHARDS * COLS), BF),
            vm((SHARDS * COLS, COLS), BF),
            vm((3, ROWS + 16, 2 * COLS), BF),
            vm((2 * ROWS, COLS), BF),
            vm((2 * ROWS, COLS), BF),
            vm((3, 2 * ROWS, ROWS), F32),
            vm((2, ROWS, COLS), BF),
            vm((ROWS, COLS), BF),
            vm((2, 3, ROWS, COLS), BF),
            vm((2, ROWS, COLS), BF),
            vm((2, ROWS, COLS), BF),
            vm((3, ROWS, COLS), BF),
            vm((2, SHARDS, BLOCK, COLS), BF),
            vm((2, NZ, LATE_PART, COLS), BF),
            vm((NY, 2, BLOCK - TOPS[1], COLS), BF),
            vm((2, NY, LATE_PART, COLS), BF),
            vm((NZ, 2, BLOCK - TOPS[1], COLS), BF),
            vm((2, SHARDS, BLOCK, COLS), BF),
            vm((NX, 2, ROWS, COLS), BF),
            vm((NX, 2, ROWS, COLS), BF),
            vm((ROWS, COLS), BF),
            vm((ROWS, COLS), BF),
            vm((ROWS, COLS), BF),
            vm((NZ, TOPS[0], COLS), BF),
            vm((NY, 2, BLOCK - TOPS[0], COLS), BF),
            vm((NY, TOPS[0], COLS), BF),
            vm((2, BLOCK - TOPS[0], COLS), BF),
            vm((NZ, PIECE, COLS), BF),
            vm((POOL_ROWS, COLS), BF),
            pltpu.SMEM((1,), jnp.int32),
            pltpu.SMEM((2, 3), jnp.int32),
            pltpu.SemaphoreType.DMA((5,)),
            pltpu.SemaphoreType.DMA((N_POOLS,)),
            pltpu.SemaphoreType.DMA((N_GROUPS,)),
            pltpu.SemaphoreType.DMA((6,)),
            pltpu.SemaphoreType.DMA((3,)),
        ],
        compiler_params=params,
        cost_estimate=pl.CostEstimate(
            flops=1200000000, bytes_accessed=3000000, transcendentals=400000
        ),
    )(inputs, out_grad, w_query, w_key, w_value, w_out, live_rows, window_blocks)
    width = SHARDS * COLS
    cols = jax.ShapeDtypeStruct((SHARDS, COLS, COLS), BF)
    input_grad, grad_query, grad_key, grad_value, grad_out = pl.pallas_call(
        hand_out,
        out_shape=(
            jax.ShapeDtypeStruct((ROWS, COLS), BF),
            cols,
            cols,
            cols,
            jax.ShapeDtypeStruct((COLS, width), BF),
        ),
        in_specs=[anyspec] * 2,
        out_specs=[anyspec] * 5,
        scratch_shapes=[
            vm((ROWS, COLS), BF),
            vm((4, SHARDS, BLOCK, COLS), BF),
            pltpu.SemaphoreType.DMA((9 + SHARDS,)),
        ],
        compiler_params=pltpu.CompilerParams(vmem_limit_bytes=62 * 1024 * 1024),
        cost_estimate=pl.CostEstimate(flops=0, bytes_accessed=2200000, transcendentals=0),
    )(input_grad, fin)
    return (
        input_grad,
        grad_query.reshape(width, COLS),
        grad_key.reshape(width, COLS),
        grad_value.reshape(width, COLS),
        grad_out,
    )


def solution(mesh):
    placed = (
        P("nodes", "heads"),
        P("nodes", "heads"),
        P(None, "heads"),
        P(None, "heads"),
        P(None, "heads"),
        P("heads", None),
        P("nodes"),
        P("nodes", None),
    )
    return jax.shard_map(
        body,
        mesh=mesh,
        in_specs=placed,
        out_specs=(
            P("nodes", "heads"),
            P(None, "heads"),
            P(None, "heads"),
            P(None, "heads"),
            P("heads", None),
        ),
        check_vma=False,
    )
```
